512 devices in a mesh: outer: 16 (over z, core), inner: 8 (over y), chan: 4 (over x).
Axes of the slice: x: 4, y: 8, z: 8, core: 2. Of those that a mesh axis runs over, the one named last changes fastest.
Arguments:
- q_stream: bfloat16 [16384, 4096], P(('outer', 'inner'), 'chan'), may hold values from -6 to 6
- k_stream: bfloat16 [16384, 4096], P(('outer', 'inner'), 'chan'), may hold values from -6 to 6
- v_stream: bfloat16 [16384, 4096], P(('outer', 'inner'), 'chan'), may hold values from -6 to 6
- filter_taps: bfloat16 [16384, 4096], P(('outer', 'inner'), 'chan'), may hold values from -0.046875 to 0.046875
- skip_gain: float32 [4096], P('chan'), may hold values from 0.3 to 1.5
- out_weight: bfloat16 [4096, 4096], P('chan', 'inner'), may hold values from -0.09375 to 0.09375
Outputs:
- layer_out: bfloat16 [16384, 4096], P(('outer', 'chan'), 'inner')
The draws below stay inside these ranges and needn't reach their ends.
All inputs are finite; a program needn't handle non-finite values.
Results may differ from the reference program's by a relative error of at most 0.013.
Values may be sent and summed in bfloat16 or wider, within the bound.
A program may use at most 64 MiB of HBM per device.

```python
import math
import jax
import jax.numpy as jnp
from jax import lax

D = 4096
SEQ = 16384


def block_levels(rng, extent, pieces, low, high):
    def one(dim, shards_of):
        draws = jax.random.uniform(jax.random.fold_in(jax.random.fold_in(rng, 6), dim), (shards_of,), jnp.float32, low / len(pieces), high / len(pieces))
        return jnp.repeat(jnp.exp(draws), extent[dim] // shards_of).reshape((-1,) + (1,) * (len(extent) - dim - 1))

    gain = one(*pieces[0])
    for cut in pieces[1:]:
        gain = gain * one(*cut)
    return gain


def gaussian(own_key, shape, spread, reach, shards=(), held_as=jnp.bfloat16):
    factor_of = block_levels(own_key, shape, shards, -0.22, 0.18) if shards else 1.0
    values = jax.random.normal(own_key, shape, jnp.float32) * spread * factor_of
    return jnp.minimum(jnp.maximum(values, -reach), reach).astype(held_as)


def setup_inputs(seed: int = 0) -> dict:
    key_of = jax.random.split(jax.random.key(seed), 7)
    q_stream = gaussian(key_of[0], (SEQ, D), 1.0, 6.0, ((0, 128), (1, 4)))
    k_stream = gaussian(key_of[1], (SEQ, D), 1.0, 6.0, ((0, 128), (1, 4)))
    v_stream = gaussian(key_of[2], (SEQ, D), 1.0, 6.0, ((0, 128), (1, 4)))
    filter_taps = gaussian(key_of[3], (SEQ, D), SEQ ** -0.5, 0.046875, ((0, 128), (1, 4)))
    skip_gain = jnp.clip(jnp.exp(math.log(1.5) - 1.60943787 * jax.random.uniform(key_of[4], (D,), jnp.float32) ** block_levels(key_of[4], (D,), ((0, 4),), -0.2, 0.2)), 0.3, 1.5)
    out_weight = gaussian(key_of[5], (D, D), D ** -0.5, 0.09375, ((0, 4), (1, 8)))
    return dict(q_stream=q_stream, k_stream=k_stream, v_stream=v_stream, filter_taps=filter_taps, skip_gain=skip_gain, out_weight=out_weight)


def reference(q_stream, k_stream, v_stream, filter_taps, skip_gain, out_weight):
    product = (k_stream.astype(jnp.float32) * v_stream.astype(jnp.float32)).astype(jnp.bfloat16)
    width = min(D, 256)
    groups = D // width
    length = 2 * SEQ

    def convolve(pair):
        signal, taps = pair
        spectrum = jnp.fft.rfft(signal.astype(jnp.float32), n=length, axis=0) * jnp.fft.rfft(taps.astype(jnp.float32), n=length, axis=0)
        return jnp.fft.irfft(spectrum, n=length, axis=0)[:SEQ].astype(jnp.float32)

    signal_blocks = product.reshape(SEQ, groups, width).transpose(1, 0, 2)
    tap_blocks = filter_taps.reshape(SEQ, groups, width).transpose(1, 0, 2)
    conv = lax.map(convolve, (signal_blocks, tap_blocks))
    conv = conv.transpose(1, 0, 2).reshape(SEQ, D).astype(jnp.bfloat16)
    mixed = conv.astype(jnp.float32) + skip_gain[None, :] * product.astype(jnp.float32)
    gated = (q_stream.astype(jnp.float32) * mixed).astype(jnp.bfloat16)
    return jnp.dot(gated, out_weight, preferred_element_type=jnp.float32).astype(jnp.bfloat16)
```

```python
import functools

import jax
import jax.numpy as jnp
import numpy as np
from jax import lax
from jax.experimental import pallas as pl
from jax.experimental.pallas import tpu as pltpu
from jax.sharding import PartitionSpec as P

MESH = pl.DeviceIdType.MESH
F32 = jnp.float32
BF16 = jnp.bfloat16


def split_table(values):
    high = values.astype(np.float32).astype(jnp.bfloat16)
    low = (values - high.astype(np.float64)).astype(np.float32).astype(jnp.bfloat16)
    return high, low


@functools.lru_cache(maxsize=None)
def tables(slabs, tok):
    coarse = 2 * slabs
    total = coarse * tok
    rows = slabs + 1
    padded = -(-rows // 16) * 16
    k = np.arange(padded)
    live = (k < rows).astype(np.float64)
    angle = 2 * np.pi * ((k[:, None] * np.arange(slabs)[None, :]) % coarse) / coarse
    cos, sin = np.cos(angle) * live[:, None], np.sin(angle) * live[:, None]
    section = np.concatenate(split_table(np.concatenate([cos, -sin], axis=0)), axis=1)
    weight = np.where((k == 0) | (k == slabs), 1.0, 2.0) / total
    back = np.concatenate([(cos * weight[:, None]).T, (-sin * weight[:, None]).T], axis=1)
    back = np.stack(split_table(back))
    turn = 2 * np.pi * ((k[:, None] * np.arange(tok)[None, :]) % total) / total
    twist = np.stack([np.cos(turn), np.sin(turn)]).astype(np.float32)
    m = np.arange(tok)
    fine = 2 * np.pi * ((m[:, None] * m[None, :]) % tok) / tok
    c, s = np.cos(fine), np.sin(fine)
    forth = np.stack(split_table(np.block([[c, -s], [s, c]])))
    inverse = np.stack(split_table(np.block([[c, s], [-s, c]])))
    return section, twist, forth, inverse, back


def dot(a, b):
    return jnp.dot(a, b, preferred_element_type=F32)


def halves(x):
    high = x.astype(BF16)
    return high, (x - high.astype(F32)).astype(BF16)


def dot3(x, table):
    high, low = halves(x)
    return dot(high, table[0]) + (dot(high, table[1]) + dot(low, table[0]))


def near_first(n):
    order = [0]
    for d in range(1, n // 2):
        order += [d, n - d]
    return order + [n // 2]


def kernel(
    sizes,
    q_hbm, k_hbm, v_hbm, taps_hbm, skip_ref, w_hbm,
    section_ref, twist_ref, forth_ref, inverse_ref, back_ref,
    out_ref,
    k_buf, v_buf, taps_buf, w_buf,
    send1, recv1, recv2, signals, send2, recv3, conv_rows, skipped, q_recv, gated, send_part, recv_part,
    load_sem, y_send, y_recv, q_send, q_recv_sem, z_send, z_recv, b_send, b_recv, g_send, g_recv, p_send, p_recv,
):
    outer_n, inner_n, chan_n, tok, per = sizes
    block = outer_n * per
    o, i, c = lax.axis_index("outer"), lax.axis_index("inner"), lax.axis_index("chan")
    order = near_first(inner_n)
    waves = [(0, 1)]
    while waves[-1][1] < inner_n:
        low = waves[-1][1]
        waves.append((low, inner_n if low + 3 >= inner_n else low + 2))
    piece = inner_n * tok // chan_n
    hops = [2, 1, 3, 0] if chan_n == 4 else list(range(1, chan_n)) + [0]

    def at_inner(d):
        return lax.rem(i + d, inner_n)

    def at_outer(r):
        return lax.rem(o + r, outer_n)

    def at_chan(d):
        return lax.rem(c + d, chan_n)

    def cols(index):
        return pl.ds(pl.multiple_of(index * block, block), block)

    barrier = pltpu.get_barrier_semaphore()
    for d in range(1, inner_n):
        pl.semaphore_signal(barrier, inc=1, device_id={"inner": at_inner(d)}, device_id_type=MESH)
    for r in range(1, outer_n):
        pl.semaphore_signal(barrier, inc=1, device_id={"outer": at_outer(r)}, device_id_type=MESH)
    for d in range(1, chan_n):
        pl.semaphore_signal(barrier, inc=1, device_id={"chan": at_chan(d)}, device_id_type=MESH)

    loads = [
        pltpu.make_async_copy(k_hbm, k_buf, load_sem.at[0]),
        pltpu.make_async_copy(v_hbm, v_buf, load_sem.at[1]),
        pltpu.make_async_copy(taps_hbm, taps_buf, load_sem.at[2]),
        pltpu.make_async_copy(w_hbm, w_buf, load_sem.at[3]),
        pltpu.make_async_copy(q_hbm.at[:, cols(i)], q_recv.at[i], load_sem.at[4]),
    ]
    for load in loads:
        load.start()
    for load in loads[:3]:
        load.wait()

    def pack(index):
        span = cols(index)
        product = (k_buf[:, span].astype(F32) * v_buf[:, span].astype(F32)).astype(BF16).astype(F32)
        product = product.T.reshape(outer_n, per, tok)
        taps = taps_buf[:, span].astype(F32).T.reshape(outer_n, per, tok)
        return jnp.concatenate([product, taps], axis=1).astype(BF16)

    def y_copy(slot, d):
        return pltpu.make_async_remote_copy(
            src_ref=send1.at[slot], dst_ref=recv1.at[order.index((inner_n - d) % inner_n)],
            send_sem=y_send.at[slot], recv_sem=y_recv.at[order.index((inner_n - d) % inner_n)],
            device_id={"inner": at_inner(d)}, device_id_type=MESH,
        )

    recv1[0] = pack(i)
    for slot in range(1, inner_n):
        send1[slot] = pack(at_inner(order[slot]))
        if slot == 1:
            pl.semaphore_wait(barrier, inner_n + outer_n + chan_n - 3)
        y_copy(slot, order[slot]).start()

    def z_copy(wave, r):
        low, high = waves[wave]
        return pltpu.make_async_remote_copy(
            src_ref=recv1.at[pl.ds(low, high - low), at_outer(r)],
            dst_ref=recv2.at[o, pl.ds(low, high - low)],
            send_sem=z_send.at[wave, r], recv_sem=z_recv.at[wave, outer_n - r],
            device_id={"outer": at_outer(r)}, device_id_type=MESH,
        )

    def z_arrival(wave, r):
        low, high = waves[wave]
        here = recv2.at[at_outer(r), pl.ds(low, high - low)]
        return pltpu.make_async_remote_copy(
            src_ref=here, dst_ref=here,
            send_sem=z_send.at[wave, r], recv_sem=z_recv.at[wave, r],
            device_id={"outer": at_outer(r)}, device_id_type=MESH,
        )

    def q_copy(d):
        return pltpu.make_async_remote_copy(
            src_ref=q_hbm.at[:, cols(at_inner(d))], dst_ref=q_recv.at[i],
            send_sem=q_send.at[d], recv_sem=q_recv_sem.at[inner_n - d],
            device_id={"inner": at_inner(d)}, device_id_type=MESH,
        )

    for wave, (low, high) in enumerate(waves):
        for slot in range(low, high):
            if slot > 0:
                y_copy(slot, (inner_n - order[slot]) % inner_n).wait_recv()

        def z_start(r, carry, wave=wave):
            z_copy(wave, r).start()
            return carry

        lax.fori_loop(1, outer_n, z_start, 0)
    for d in order[1:]:
        q_copy(d).start()

    gain = skip_ref[:, cols(i)]
    for slot in range(inner_n):
        both = recv1[slot].astype(F32)
        product = both[:, :per].reshape(block, tok).T
        at = pl.multiple_of(at_inner(order[slot]) * tok, tok)
        skipped[pl.ds(at, tok), :] = product * gain

    for wave, (low, high) in enumerate(waves):

        def z_wait(r, carry, wave=wave):
            z_arrival(wave, r).wait_recv()
            return carry

        lax.fori_loop(1, outer_n, z_wait, 0)
        for slot in range(low, high):
            recv2[o, slot] = recv1[slot, o]
        for slot in range(low, high):
            place = at_inner(order[slot])
            for source in range(outer_n):
                row = pl.multiple_of((source * inner_n + place) * (2 * per), 2 * per)
                signals[pl.ds(row, 2 * per), :] = recv2[source, slot].astype(F32)

    slabs = outer_n * inner_n
    padded = twist_ref.shape[1]
    cos_twist, sin_twist = twist_ref[0], twist_ref[1]

    def wide(table, times):
        return jnp.concatenate([table] * times, axis=1)

    def convolve(first):
        both = []
        for channel in (first, first + 1):
            for kind in range(2):
                both.append(signals[pl.ds(channel + kind * per, slabs, stride=2 * per), :].astype(BF16))
        x = jnp.concatenate(both, axis=1)
        y = dot(section_ref[...], jnp.concatenate([x, x], axis=0))
        real, imag = y[:padded], y[padded:]
        cos4, sin4 = wide(cos_twist, 4), wide(sin_twist, 4)
        turned_real = real * cos4 + imag * sin4
        turned_imag = imag * cos4 - real * sin4
        stacked = jnp.concatenate(
            [
                jnp.concatenate([t[:, n * tok : (n + 1) * tok] for t in (turned_real, turned_imag)], axis=1)
                for n in range(4)
            ],
            axis=0,
        )
        spec = dot3(stacked, forth_ref)
        prods = []
        for n in range(2):
            a = spec[2 * n * padded : (2 * n + 1) * padded]
            b = spec[(2 * n + 1) * padded : (2 * n + 2) * padded]
            ar, ai, br, bi = a[:, :tok], a[:, tok:], b[:, :tok], b[:, tok:]
            prods.append(jnp.concatenate([ar * br - ai * bi, ar * bi + ai * br], axis=1))
        ret = dot3(jnp.concatenate(prods, axis=0), inverse_ref)
        ups = []
        for n in range(2):
            r = ret[n * padded : (n + 1) * padded]
            rr, ri = r[:, :tok], r[:, tok:]
            ups.append(
                jnp.concatenate([rr * cos_twist - ri * sin_twist, ri * cos_twist + rr * sin_twist], axis=0)
            )
        high, low = halves(jnp.concatenate(ups, axis=1))
        conv = dot(back_ref[0], high) + (dot(back_ref[1], high) + dot(back_ref[0], low))
        conv = [conv[:, n * tok : (n + 1) * tok].reshape(outer_n, inner_n, tok) for n in range(2)]
        return jnp.concatenate(conv, axis=1).astype(BF16)

    for pair in range(per // 2):
        send2[:, pl.ds(pair * 2 * inner_n, 2 * inner_n), :] = convolve(2 * pair)

    def b_copy(r):
        return pltpu.make_async_remote_copy(
            src_ref=send2.at[at_outer(r)], dst_ref=recv3.at[o],
            send_sem=b_send.at[r], recv_sem=b_recv.at[outer_n - r],
            device_id={"outer": at_outer(r)}, device_id_type=MESH,
        )

    def b_arrival(r):
        here = recv3.at[at_outer(r)]
        return pltpu.make_async_remote_copy(
            src_ref=here, dst_ref=here, send_sem=b_send.at[r], recv_sem=b_recv.at[r],
            device_id={"outer": at_outer(r)}, device_id_type=MESH,
        )

    def b_start(r, carry):
        b_copy(r).start()
        return carry

    def b_wait(r, carry):
        b_arrival(r).wait_recv()
        return carry

    lax.fori_loop(1, outer_n, b_start, 0)
    recv3[o] = send2[o]
    loads[3].wait()
    loads[4].wait()
    for d in range(1, inner_n):
        q_copy(inner_n - d).wait_recv()
    lax.fori_loop(1, outer_n, b_wait, 0)

    for source in range(outer_n):
        conv_rows[pl.ds(source * per * inner_n, per * inner_n), :] = recv3[source].astype(F32)
    for slab in range(inner_n):
        conv = conv_rows[pl.ds(slab, block, stride=inner_n), :].T
        span = pl.ds(slab * tok, tok)
        gated[i, span, :] = (q_recv[slab].astype(F32) * (conv + skipped[span, :])).astype(BF16)

    def reach(way, u):
        longer = inner_n // 2
        return longer if (u + way) % 2 == 0 else inner_n - 1 - longer

    def tokens_of(u):
        return pl.ds(pl.multiple_of(at_chan(hops[u]) * piece, piece), piece)

    def g_copy(way, u, r):
        step = 1 if way == 0 else inner_n - 1
        source = at_inner((inner_n - step) * (r - 1) % inner_n)
        part = gated.at[source, tokens_of(u)]
        return pltpu.make_async_remote_copy(
            src_ref=part, dst_ref=part,
            send_sem=g_send.at[way, u, r - 1], recv_sem=g_recv.at[way, u, r - 1],
            device_id={"inner": at_inner(step)}, device_id_type=MESH,
        )

    def g_arrival(way, u, r):
        step = 1 if way == 0 else inner_n - 1
        source = at_inner((inner_n - step) * r % inner_n)
        part = gated.at[source, tokens_of(u)]
        return pltpu.make_async_remote_copy(
            src_ref=part, dst_ref=part,
            send_sem=g_send.at[way, u, r - 1], recv_sem=g_recv.at[way, u, r - 1],
            device_id={"inner": at_inner(step)}, device_id_type=MESH,
        )

    def p_copy(u):
        return pltpu.make_async_remote_copy(
            src_ref=send_part.at[u], dst_ref=recv_part.at[u],
            send_sem=p_send.at[u], recv_sem=p_recv.at[u],
            device_id={"chan": at_chan(hops[u])}, device_id_type=MESH,
        )

    longest = inner_n // 2
    events = {}
    for u in range(chan_n):
        for r in range(1, longest + 2):
            events.setdefault(2 * u + r, []).append((u, r))
    for key in sorted(events):
        for u, r in events[key]:
            for way in range(2):
                if 1 < r <= reach(way, u) + 1:
                    g_arrival(way, u, r - 1).wait_recv()
                if r <= reach(way, u):
                    g_copy(way, u, r).start()
            if r == longest + 1:
                left = jnp.concatenate([gated[n, tokens_of(u), :] for n in range(inner_n)], axis=1)
                part = dot(left, w_buf[...])
                if u < chan_n - 1:
                    send_part[u] = part.astype(BF16)
                    p_copy(u).start()
                else:
                    total = part
                    for n in range(chan_n - 1):
                        p_copy(n).wait_recv()
                        total = total + recv_part[n].astype(F32)
                    out_ref[...] = total.astype(BF16)

    for slot in range(1, inner_n):
        y_copy(slot, order[slot]).wait_send()
    for d in range(1, inner_n):
        q_copy(d).wait_send()

    def sent(r, carry):
        for wave in range(len(waves)):
            z_copy(wave, r).wait_send()
        b_copy(r).wait_send()
        return carry

    lax.fori_loop(1, outer_n, sent, 0)
    for u in range(chan_n):
        for way in range(2):
            for r in range(1, reach(way, u) + 1):
                g_copy(way, u, r).wait_send()
        if u < chan_n - 1:
            p_copy(u).wait_send()


def local(q_stream, k_stream, v_stream, filter_taps, skip_gain, out_weight):
    tok, chans = k_stream.shape
    outer_n, inner_n, chan_n = (lax.axis_size(a) for a in ("outer", "inner", "chan"))
    slabs = outer_n * inner_n
    per = chans // slabs
    block = outer_n * per
    width = out_weight.shape[1]
    coarse = inner_n * tok
    piece = coarse // chan_n
    held = tables(slabs, tok)
    sizes = (outer_n, inner_n, chan_n, tok, per)
    waves = max(2, inner_n // 2)
    dma = pltpu.SemaphoreType.DMA
    any_spec, vmem = pl.BlockSpec(memory_space=pl.ANY), pl.BlockSpec(memory_space=pltpu.VMEM)
    return pl.pallas_call(
        functools.partial(kernel, sizes),
        out_shape=jax.ShapeDtypeStruct((piece, width), BF16),
        in_specs=[any_spec] * 4 + [vmem, any_spec] + [vmem] * 5,
        out_specs=vmem,
        scratch_shapes=[
            pltpu.VMEM((tok, chans), BF16),
            pltpu.VMEM((tok, chans), BF16),
            pltpu.VMEM((tok, chans), BF16),
            pltpu.VMEM((chans, width), BF16),
            pltpu.VMEM((inner_n, outer_n, 2 * per, tok), BF16),
            pltpu.VMEM((inner_n, outer_n, 2 * per, tok), BF16),
            pltpu.VMEM((outer_n, inner_n, 2 * per, tok), BF16),
            pltpu.VMEM((slabs * 2 * per, tok), F32),
            pltpu.VMEM((outer_n, per * inner_n, tok), BF16),
            pltpu.VMEM((outer_n, per * inner_n, tok), BF16),
            pltpu.VMEM((outer_n * per * inner_n, tok), F32),
            pltpu.VMEM((coarse, block), F32),
            pltpu.VMEM((inner_n, tok, block), BF16),
            pltpu.VMEM((inner_n, coarse, block), BF16),
            pltpu.VMEM((chan_n - 1, piece, width), BF16),
            pltpu.VMEM((chan_n - 1, piece, width), BF16),
            dma((5,)),
            dma((inner_n,)),
            dma((inner_n,)),
            dma((inner_n,)),
            dma((inner_n,)),
            dma((waves, outer_n)),
            dma((waves, outer_n)),
            dma((outer_n,)),
            dma((outer_n,)),
            dma((2, chan_n, inner_n // 2)),
            dma((2, chan_n, inner_n // 2)),
            dma((chan_n - 1,)),
            dma((chan_n - 1,)),
        ],
        compiler_params=pltpu.CompilerParams(
            collective_id=0, has_side_effects=True, vmem_limit_bytes=40 * 1024 * 1024
        ),
    )(q_stream, k_stream, v_stream, filter_taps, skip_gain[None, :], out_weight, *(jnp.asarray(t) for t in held))


def solution(mesh):
    return jax.shard_map(
        local,
        mesh=mesh,
        in_specs=(
            P(("outer", "inner"), "chan"),
            P(("outer", "inner"), "chan"),
            P(("outer", "inner"), "chan"),
            P(("outer", "inner"), "chan"),
            P("chan"),
            P("chan", "inner"),
        ),
        out_specs=P(("outer", "chan"), "inner"),
        check_vma=False,
    )
```

```python
import functools

import jax
import jax.numpy as jnp
import numpy as np
from jax import lax
from jax.experimental import pallas as pl
from jax.experimental.pallas import tpu as pltpu
from jax.sharding import PartitionSpec as P

MESH = pl.DeviceIdType.MESH
F32 = jnp.float32
BF16 = jnp.bfloat16
PARTS = 4
RING_LAG = 0.6


def split_table(values):
    high = values.astype(np.float32).astype(jnp.bfloat16)
    low = (values - high.astype(np.float64)).astype(np.float32).astype(jnp.bfloat16)
    return high, low


@functools.lru_cache(maxsize=None)
def tables(slabs, tok):
    coarse = 2 * slabs
    total = coarse * tok
    rows = slabs + 1
    padded = -(-rows // 16) * 16
    k = np.arange(padded)
    live = (k < rows).astype(np.float64)
    angle = 2 * np.pi * ((k[:, None] * np.arange(slabs)[None, :]) % coarse) / coarse
    cos, sin = np.cos(angle) * live[:, None], np.sin(angle) * live[:, None]
    section = np.concatenate(split_table(np.concatenate([cos, -sin], axis=0)), axis=1)
    weight = np.where((k == 0) | (k == slabs), 1.0, 2.0) / total
    back = np.concatenate([(cos * weight[:, None]).T, (-sin * weight[:, None]).T], axis=1)
    back = np.stack(split_table(back))
    turn = 2 * np.pi * ((k[:, None] * np.arange(tok)[None, :]) % total) / total
    twist = np.stack([np.cos(turn), np.sin(turn)]).astype(np.float32)
    m = np.arange(tok)
    fine = 2 * np.pi * ((m[:, None] * m[None, :]) % tok) / tok
    c, s = np.cos(fine), np.sin(fine)
    forth = np.stack(split_table(np.block([[c, -s], [s, c]])))
    inverse = np.stack(split_table(np.block([[c, s], [-s, c]])))
    return section, twist, forth, inverse, back


def dot(a, b):
    return jnp.dot(a, b, preferred_element_type=F32)


def halves(x):
    high = x.astype(BF16)
    return high, (x - high.astype(F32)).astype(BF16)


def dot3(x, table):
    high, low = halves(x)
    return dot(high, table[0]) + (dot(high, table[1]) + dot(low, table[0]))


def near_first(n):
    order = [0]
    for d in range(1, n // 2):
        order += [d, n - d]
    return order + [n // 2]


def kernel(
    sizes,
    q_hbm, k_hbm, v_hbm, taps_hbm, skip_hbm, w_hbm,
    section_hbm, twist_hbm, forth_hbm, inverse_hbm, back_hbm,
    out_ref,
    k_buf, v_buf, taps_buf, skip_ref, w_buf, section_ref, twist_ref, forth_ref, inverse_ref, back_ref,
    send1, recv1, recv2, signals, send2, recv3, conv_rows, q_recv, folded_p, folded_q, gate_p, gate_q,
    gx, gated, w_rows, weights, total,
    load_sem, y_send, y_recv, q_send, q_recv_sem, z_send, z_recv, b_send, b_recv, x_send, x_recv,
    g_send, g_recv, w_send, w_recv, f_send, f_recv,
):
    outer_n, inner_n, chan_n, tok, per, parts = sizes
    slabs = outer_n * inner_n
    block = outer_n * per
    each = per // parts
    o, i, c = lax.axis_index("outer"), lax.axis_index("inner"), lax.axis_index("chan")
    order = near_first(inner_n)
    waves = [(0, 1)]
    while waves[-1][1] < inner_n:
        low = waves[-1][1]
        waves.append((low, inner_n if low + 3 >= inner_n else low + 2))
    piece = inner_n * tok // chan_n
    near = inner_n // chan_n
    core = lax.rem(o, 2)
    sibling = o + 1 - 2 * core

    def at_inner(d):
        return lax.rem(i + d, inner_n)

    def at_outer(r):
        return lax.rem(o + r, outer_n)

    def at_chan(d):
        return lax.rem(c + d, chan_n)

    def cols(index):
        return pl.ds(pl.multiple_of(index * block, block), block)

    barrier = pltpu.get_barrier_semaphore()
    for d in range(1, inner_n):
        pl.semaphore_signal(barrier, inc=1, device_id={"inner": at_inner(d)}, device_id_type=MESH)
    for r in range(1, outer_n):
        pl.semaphore_signal(barrier, inc=1, device_id={"outer": at_outer(r)}, device_id_type=MESH)
    for d in range(1, chan_n):
        pl.semaphore_signal(barrier, inc=1, device_id={"chan": at_chan(d)}, device_id_type=MESH)

    loads = [
        pltpu.make_async_copy(k_hbm, k_buf, load_sem.at[0]),
        pltpu.make_async_copy(v_hbm, v_buf, load_sem.at[1]),
        pltpu.make_async_copy(taps_hbm, taps_buf, load_sem.at[2]),
        pltpu.make_async_copy(q_hbm.at[:, cols(i)], q_recv.at[i], load_sem.at[3]),
        pltpu.make_async_copy(skip_hbm, skip_ref, load_sem.at[4]),
        pltpu.make_async_copy(section_hbm, section_ref, load_sem.at[5]),
        pltpu.make_async_copy(twist_hbm, twist_ref, load_sem.at[6]),
        pltpu.make_async_copy(forth_hbm, forth_ref, load_sem.at[7]),
        pltpu.make_async_copy(inverse_hbm, inverse_ref, load_sem.at[8]),
        pltpu.make_async_copy(back_hbm, back_ref, load_sem.at[9]),
        pltpu.make_async_copy(w_hbm, w_buf, load_sem.at[10]),
    ]
    for load in loads:
        load.start()
    for load in loads[:3]:
        load.wait()

    def pack(index):
        span = cols(index)
        product = (k_buf[:, span].astype(F32) * v_buf[:, span].astype(F32)).astype(BF16).astype(F32)
        product = product.T.reshape(outer_n, per, tok)
        taps = taps_buf[:, span].astype(F32).T.reshape(outer_n, per, tok)
        return jnp.concatenate([product, taps], axis=1).astype(BF16)

    def y_copy(slot, d):
        return pltpu.make_async_remote_copy(
            src_ref=send1.at[slot], dst_ref=recv1.at[order.index((inner_n - d) % inner_n)],
            send_sem=y_send.at[slot], recv_sem=y_recv.at[order.index((inner_n - d) % inner_n)],
            device_id={"inner": at_inner(d)}, device_id_type=MESH,
        )

    recv1[0] = pack(i)
    for slot in range(1, inner_n):
        send1[slot] = pack(at_inner(order[slot]))
        if slot == 1:
            pl.semaphore_wait(barrier, inner_n + outer_n + chan_n - 3)
        y_copy(slot, order[slot]).start()

    def z_copy(wave, r):
        low, high = waves[wave]
        return pltpu.make_async_remote_copy(
            src_ref=recv1.at[pl.ds(low, high - low), at_outer(r)],
            dst_ref=recv2.at[o, pl.ds(low, high - low)],
            send_sem=z_send.at[wave, r], recv_sem=z_recv.at[wave, outer_n - r],
            device_id={"outer": at_outer(r)}, device_id_type=MESH,
        )

    def z_arrival(wave, r):
        low, high = waves[wave]
        here = recv2.at[at_outer(r), pl.ds(low, high - low)]
        return pltpu.make_async_remote_copy(
            src_ref=here, dst_ref=here,
            send_sem=z_send.at[wave, r], recv_sem=z_recv.at[wave, r],
            device_id={"outer": at_outer(r)}, device_id_type=MESH,
        )

    def q_copy(d):
        return pltpu.make_async_remote_copy(
            src_ref=q_hbm.at[:, cols(at_inner(d))], dst_ref=q_recv.at[i],
            send_sem=q_send.at[d], recv_sem=q_recv_sem.at[inner_n - d],
            device_id={"inner": at_inner(d)}, device_id_type=MESH,
        )

    def z_start(wave):
        def start(r, carry):
            z_copy(wave, r).start()
            return carry

        lax.fori_loop(1, outer_n, start, 0)

    z_start(0)

    for load in loads[3:]:
        load.wait()
    for n in range(w_rows.shape[0]):
        span = pl.ds(n * w_rows.shape[2], w_rows.shape[2])
        w_rows[n] = w_buf[:, span].astype(F32)
        for cc in range(per):
            rows = w_rows[n, pl.ds(cc, slabs, stride=per), :]
            weights[c, cc // each, span, pl.ds(cc % each * slabs, slabs)] = rows.T.astype(BF16)
    mine = pl.ds(core * (parts // 2), parts // 2)

    def w_copy(d):
        held = weights.at[c, mine]
        return pltpu.make_async_remote_copy(
            src_ref=held, dst_ref=held, send_sem=w_send.at[d], recv_sem=w_recv.at[chan_n - d],
            device_id={"chan": at_chan(d)}, device_id_type=MESH,
        )

    def f_copy(d, half):
        held = weights.at[at_chan(d), pl.ds(half * (parts // 2), parts // 2)]
        return pltpu.make_async_remote_copy(
            src_ref=held, dst_ref=held, send_sem=f_send.at[d], recv_sem=f_recv.at[d],
            device_id={"outer": sibling}, device_id_type=MESH,
        )

    for d in range(1, chan_n):
        w_copy(d).start()

    gain = jnp.broadcast_to(skip_ref[:, cols(i)], (tok, block)).T

    def keep_product(slot):
        both = recv1[slot].astype(F32)
        rows = pl.ds(slot * block, block)
        folded_p[rows, :] = both[:, :per].reshape(block, tok) * gain
        place = at_inner(order[slot])
        for cc in range(per):
            gate_p[cc, place] = folded_p[pl.ds(slot * block + cc, outer_n, stride=per), :]

    for wave, (low, high) in enumerate(waves):
        if wave > 0:
            for slot in range(low, high):
                y_copy(slot, (inner_n - order[slot]) % inner_n).wait_recv()
            z_start(wave)
        for slot in range(low, high):
            keep_product(slot)
    for d in order[1:]:
        q_copy(d).start()

    for wave, (low, high) in enumerate(waves):

        def z_wait(r, carry, wave=wave):
            z_arrival(wave, r).wait_recv()
            return carry

        lax.fori_loop(1, outer_n, z_wait, 0)
        for slot in range(low, high):
            recv2[o, slot] = recv1[slot, o]
        for slot in range(low, high):
            place = at_inner(order[slot])
            for source in range(outer_n):
                row = pl.multiple_of((source * inner_n + place) * (2 * per), 2 * per)
                signals[pl.ds(row, 2 * per), :] = recv2[source, slot].astype(F32)

    padded = twist_ref.shape[1]
    cos_twist, sin_twist = twist_ref[0], twist_ref[1]

    def wide(table, times):
        return jnp.concatenate([table] * times, axis=1)

    def convolve(first):
        both = []
        for channel in (first, first + 1):
            for kind in range(2):
                both.append(signals[pl.ds(channel + kind * per, slabs, stride=2 * per), :].astype(BF16))
        x = jnp.concatenate(both, axis=1)
        y = dot(section_ref[...], jnp.concatenate([x, x], axis=0))
        real, imag = y[:padded], y[padded:]
        cos4, sin4 = wide(cos_twist, 4), wide(sin_twist, 4)
        turned_real = real * cos4 + imag * sin4
        turned_imag = imag * cos4 - real * sin4
        stacked = jnp.concatenate(
            [
                jnp.concatenate([t[:, n * tok : (n + 1) * tok] for t in (turned_real, turned_imag)], axis=1)
                for n in range(4)
            ],
            axis=0,
        )
        spec = dot3(stacked, forth_ref)
        prods = []
        for n in range(2):
            a = spec[2 * n * padded : (2 * n + 1) * padded]
            b = spec[(2 * n + 1) * padded : (2 * n + 2) * padded]
            ar, ai, br, bi = a[:, :tok], a[:, tok:], b[:, :tok], b[:, tok:]
            prods.append(jnp.concatenate([ar * br - ai * bi, ar * bi + ai * br], axis=1))
        ret = dot3(jnp.concatenate(prods, axis=0), inverse_ref)
        ups = []
        for n in range(2):
            r = ret[n * padded : (n + 1) * padded]
            rr, ri = r[:, :tok], r[:, tok:]
            ups.append(
                jnp.concatenate([rr * cos_twist - ri * sin_twist, ri * cos_twist + rr * sin_twist], axis=0)
            )
        high, low = halves(jnp.concatenate(ups, axis=1))
        conv = dot(back_ref[0], high) + (dot(back_ref[1], high) + dot(back_ref[0], low))
        conv = [conv[:, n * tok : (n + 1) * tok].reshape(outer_n, inner_n, tok) for n in range(2)]
        return jnp.concatenate(conv, axis=1).astype(BF16)

    def part_rows(h):
        return pl.ds(h * each * inner_n, each * inner_n)

    def b_copy(h, r):
        return pltpu.make_async_remote_copy(
            src_ref=send2.at[at_outer(r), part_rows(h)], dst_ref=recv3.at[o, part_rows(h)],
            send_sem=b_send.at[h, r], recv_sem=b_recv.at[h, outer_n - r],
            device_id={"outer": at_outer(r)}, device_id_type=MESH,
        )

    def b_arrival(h, r):
        here = recv3.at[at_outer(r), part_rows(h)]
        return pltpu.make_async_remote_copy(
            src_ref=here, dst_ref=here, send_sem=b_send.at[h, r], recv_sem=b_recv.at[h, r],
            device_id={"outer": at_outer(r)}, device_id_type=MESH,
        )

    for h in range(parts):
        for pair in range(h * each // 2, (h + 1) * each // 2):
            send2[:, pl.ds(pair * 2 * inner_n, 2 * inner_n), :] = convolve(2 * pair)

        def b_start(r, carry, h=h):
            b_copy(h, r).start()
            return carry

        lax.fori_loop(1, outer_n, b_start, 0)
    recv3[o] = send2[o]

    for d in range(1, inner_n):
        q_copy(inner_n - d).wait_recv()
    for slab in range(inner_n):
        folded_q[pl.ds(slab * block, block), :] = q_recv[slab].astype(F32).T
        for cc in range(per):
            gate_q[cc, slab] = folded_q[pl.ds(slab * block + cc, outer_n, stride=per), :]

    def x_copy(h, d):
        return pltpu.make_async_remote_copy(
            src_ref=gx.at[h, at_chan(d)], dst_ref=gated.at[h, c, :, i],
            send_sem=x_send.at[h, d], recv_sem=x_recv.at[h, chan_n - d],
            device_id={"chan": at_chan(d)}, device_id_type=MESH,
        )

    for h in range(parts):

        def b_wait(r, carry, h=h):
            b_arrival(h, r).wait_recv()
            return carry

        lax.fori_loop(1, outer_n, b_wait, 0)
        count = each * inner_n
        first = h * outer_n * count
        for source in range(outer_n):
            conv_rows[pl.ds(first + source * count, count), :] = recv3[source, part_rows(h), :].astype(F32)
        for e in range(each):
            cc = h * each + e
            for slab in range(inner_n):
                conv = conv_rows[pl.ds(first + e * inner_n + slab, outer_n, stride=count), :]
                value = (gate_q[cc, slab] * (conv + gate_p[cc, slab])).astype(BF16)
                gx[h, slab // near, e, :, pl.ds(slab % near * tok, tok)] = value
        for d in range(1, chan_n):
            x_copy(h, d).start()
        gated[h, c, :, i] = gx[h, c]

    for d in range(1, chan_n):
        w_copy(chan_n - d).wait_recv()
        f_copy(d, core).start()

    longest = inner_n // 2

    def reach(way, h):
        return longest if (h + way) % 2 == 0 else inner_n - 1 - longest

    def g_copy(way, h, r, arrival=False):
        step = 1 if way == 0 else inner_n - 1
        source = at_inner((inner_n - step) * (r if arrival else r - 1) % inner_n)
        held = gated.at[h, :, :, source]
        return pltpu.make_async_remote_copy(
            src_ref=held, dst_ref=held,
            send_sem=g_send.at[way, h, r - 1], recv_sem=g_recv.at[way, h, r - 1],
            device_id={"inner": at_inner(step)}, device_id_type=MESH,
        )

    events = []
    for h in range(parts):
        for r in range(1, longest + 2):
            events.append((RING_LAG * h + r, h, r))
    for _, h, r in sorted(events):
        if r == 1:
            for d in range(1, chan_n):
                x_copy(h, chan_n - d).wait_recv()
        for way in range(2):
            if 1 < r <= reach(way, h) + 1:
                g_copy(way, h, r - 1, arrival=True).wait_recv()
            if r <= reach(way, h):
                g_copy(way, h, r).start()
        if r == longest + 1:
            if h == 0:
                for d in range(1, chan_n):
                    f_copy(d, 1 - core).wait_recv()
            part = None
            for group in range(chan_n):
                left, right = weights[group, h], gated[h, group].reshape(each * slabs, near * tok)
                term = dot(left, right)
                part = term if part is None else part + term
            if h < parts - 1:
                total[...] = part if h == 0 else total[...] + part
            else:
                out_ref[...] = (total[...] + part).T.astype(BF16)

    for slot in range(1, inner_n):
        y_copy(slot, order[slot]).wait_send()
    for d in range(1, inner_n):
        q_copy(d).wait_send()

    def sent(r, carry):
        for wave in range(len(waves)):
            z_copy(wave, r).wait_send()
        for h in range(parts):
            b_copy(h, r).wait_send()
        return carry

    lax.fori_loop(1, outer_n, sent, 0)
    for d in range(1, chan_n):
        w_copy(d).wait_send()
        f_copy(d, core).wait_send()
        for h in range(parts):
            x_copy(h, d).wait_send()
    for h in range(parts):
        for way in range(2):
            for r in range(1, reach(way, h) + 1):
                g_copy(way, h, r).wait_send()


def local(q_stream, k_stream, v_stream, filter_taps, skip_gain, out_weight):
    tok, chans = k_stream.shape
    outer_n, inner_n, chan_n = (lax.axis_size(a) for a in ("outer", "inner", "chan"))
    slabs = outer_n * inner_n
    per = chans // slabs
    block = outer_n * per
    width = out_weight.shape[1]
    coarse = inner_n * tok
    piece = coarse // chan_n
    held = tables(slabs, tok)
    parts = PARTS
    each = per // parts
    lanes = min(width, 128)
    sizes = (outer_n, inner_n, chan_n, tok, per, parts)
    waves = max(2, inner_n // 2)
    dma = pltpu.SemaphoreType.DMA
    hbm = pl.BlockSpec(memory_space=pltpu.HBM)
    return pl.pallas_call(
        functools.partial(kernel, sizes),
        out_shape=jax.ShapeDtypeStruct((piece, width), BF16),
        in_specs=[hbm] * 11,
        out_specs=pl.BlockSpec(memory_space=pltpu.VMEM),
        scratch_shapes=[
            pltpu.VMEM((tok, chans), BF16),
            pltpu.VMEM((tok, chans), BF16),
            pltpu.VMEM((tok, chans), BF16),
            pltpu.VMEM((1, chans), F32),
            pltpu.VMEM((chans, width), BF16),
            *(pltpu.VMEM(t.shape, t.dtype) for t in held),
            pltpu.VMEM((inner_n, outer_n, 2 * per, tok), BF16),
            pltpu.VMEM((inner_n, outer_n, 2 * per, tok), BF16),
            pltpu.VMEM((outer_n, inner_n, 2 * per, tok), BF16),
            pltpu.VMEM((slabs * 2 * per, tok), F32),
            pltpu.VMEM((outer_n, per * inner_n, tok), BF16),
            pltpu.VMEM((outer_n, per * inner_n, tok), BF16),
            pltpu.VMEM((outer_n * per * inner_n, tok), F32),
            pltpu.VMEM((inner_n, tok, block), BF16),
            pltpu.VMEM((inner_n * block, tok), F32),
            pltpu.VMEM((inner_n * block, tok), F32),
            pltpu.VMEM((per, inner_n, outer_n, tok), F32),
            pltpu.VMEM((per, inner_n, outer_n, tok), F32),
            pltpu.VMEM((parts, chan_n, each, outer_n, piece), BF16),
            pltpu.VMEM((parts, chan_n, each, inner_n, outer_n, piece), BF16),
            pltpu.VMEM((width // lanes, chans, lanes), F32),
            pltpu.VMEM((chan_n, parts, width, each * slabs), BF16),
            pltpu.VMEM((width, piece), F32),
            dma((11,)),
            dma((inner_n,)),
            dma((inner_n,)),
            dma((inner_n,)),
            dma((inner_n,)),
            dma((waves, outer_n)),
            dma((waves, outer_n)),
            dma((parts, outer_n)),
            dma((parts, outer_n)),
            dma((parts, chan_n)),
            dma((parts, chan_n)),
            dma((2, parts, inner_n // 2)),
            dma((2, parts, inner_n // 2)),
            dma((chan_n,)),
            dma((chan_n,)),
            dma((chan_n,)),
            dma((chan_n,)),
        ],
        compiler_params=pltpu.CompilerParams(
            collective_id=0, has_side_effects=True, vmem_limit_bytes=60 * 1024 * 1024
        ),
    )(q_stream, k_stream, v_stream, filter_taps, skip_gain[None, :], out_weight, *(jnp.asarray(t) for t in held))


def solution(mesh):
    return jax.shard_map(
        local,
        mesh=mesh,
        in_specs=(
            P(("outer", "inner"), "chan"),
            P(("outer", "inner"), "chan"),
            P(("outer", "inner"), "chan"),
            P(("outer", "inner"), "chan"),
            P("chan"),
            P("chan", "inner"),
        ),
        out_specs=P(("outer", "chan"), "inner"),
        check_vma=False,
    )
```

```python
import functools

import jax
import jax.numpy as jnp
import numpy as np
from jax import lax
from jax.experimental import pallas as pl
from jax.experimental.pallas import tpu as pltpu
from jax.sharding import PartitionSpec as P

MESH = pl.DeviceIdType.MESH
F32 = jnp.float32
BF16 = jnp.bfloat16
PARTS = 4
RING_LAG = 0.3
Q_AT = 4
PASS_AT = 3


def split_table(values):
    high = values.astype(np.float32).astype(jnp.bfloat16)
    low = (values - high.astype(np.float64)).astype(np.float32).astype(jnp.bfloat16)
    return high, low


@functools.lru_cache(maxsize=None)
def tables(slabs, tok):
    coarse = 2 * slabs
    total = coarse * tok
    rows = slabs + 1
    padded = -(-rows // 16) * 16
    k = np.arange(padded)
    live = (k < rows).astype(np.float64)
    angle = 2 * np.pi * ((k[:, None] * np.arange(slabs)[None, :]) % coarse) / coarse
    cos, sin = np.cos(angle) * live[:, None], np.sin(angle) * live[:, None]
    section = np.concatenate(split_table(np.concatenate([cos, -sin], axis=0)), axis=1)
    weight = np.where((k == 0) | (k == slabs), 1.0, 2.0) / total
    back = np.concatenate([(cos * weight[:, None]).T, (-sin * weight[:, None]).T], axis=1)
    back = np.stack(split_table(back))
    turn = 2 * np.pi * ((k[:, None] * np.arange(tok)[None, :]) % total) / total
    twist = np.stack([np.cos(turn), np.sin(turn)]).astype(np.float32)
    m = np.arange(tok)
    fine = 2 * np.pi * ((m[:, None] * m[None, :]) % tok) / tok
    c, s = np.cos(fine), np.sin(fine)
    forth = np.stack(split_table(np.block([[c, -s], [s, c]])))
    inverse = np.stack(split_table(np.block([[c, s], [-s, c]])))
    return section, twist, forth, inverse, back


def pick_table(outer_n, per):
    block = outer_n * per
    device, signal, channel = np.meshgrid(np.arange(outer_n), np.arange(2), np.arange(per), indexing="ij")
    column = (signal * block + device * per + channel).reshape(-1)
    return (column[:, None] == np.arange(2 * block)[None, :]).astype(np.float32).astype(jnp.bfloat16)


def dot(a, b):
    return jnp.dot(a, b, preferred_element_type=F32)


def halves(x):
    high = x.astype(BF16)
    return high, (x - high.astype(F32)).astype(BF16)


def dot3(x, table):
    high, low = halves(x)
    return dot(high, table[0]) + (dot(high, table[1]) + dot(low, table[0]))


def near_first(n):
    order = [0]
    for d in range(1, n // 2):
        order += [d, n - d]
    return order + [n // 2]


def kernel(
    sizes,
    q_hbm, k_hbm, v_hbm, taps_hbm, skip_hbm, w_hbm,
    section_hbm, twist_hbm, forth_hbm, inverse_hbm, back_hbm, pick_hbm,
    out_ref,
    k_buf, v_buf, taps_buf, skip_ref, w_buf, section_ref, twist_ref, forth_ref, inverse_ref, back_ref, pick_ref,
    send1, recv2, signals, send2, recv3, conv_rows, q_recv, gains, folded, gate_q,
    gx, gated, w_rows, weights, total,
    load_sem, ready, d_send, d_recv, q_send, q_recv_sem, b_send, b_recv, x_send, x_recv,
    g_send, g_recv, w_send, w_recv, f_send, f_recv,
):
    outer_n, inner_n, chan_n, tok, per, parts = sizes
    slabs = outer_n * inner_n
    block = outer_n * per
    each = per // parts
    o, i, c = lax.axis_index("outer"), lax.axis_index("inner"), lax.axis_index("chan")
    order = near_first(inner_n)
    near = inner_n // chan_n
    core = lax.rem(o, 2)
    sibling = o + 1 - 2 * core

    def at_inner(d):
        return lax.rem(i + d, inner_n)

    def at_outer(r):
        return lax.rem(o + r, outer_n)

    def at_chan(d):
        return lax.rem(c + d, chan_n)

    def cols(index):
        return pl.ds(pl.multiple_of(index * block, block), block)

    barrier = pltpu.get_barrier_semaphore()
    for d in range(1, inner_n):
        pl.semaphore_signal(barrier, inc=1, device_id={"inner": at_inner(d)}, device_id_type=MESH)
    for r in range(1, outer_n):
        pl.semaphore_signal(barrier, inc=1, device_id={"outer": at_outer(r)}, device_id_type=MESH)
    for d in range(1, chan_n):
        pl.semaphore_signal(barrier, inc=1, device_id={"chan": at_chan(d)}, device_id_type=MESH)

    loads = [
        pltpu.make_async_copy(k_hbm, k_buf, load_sem.at[0]),
        pltpu.make_async_copy(v_hbm, v_buf, load_sem.at[1]),
        pltpu.make_async_copy(taps_hbm, taps_buf, load_sem.at[2]),
        pltpu.make_async_copy(pick_hbm, pick_ref, load_sem.at[11]),
        pltpu.make_async_copy(q_hbm.at[:, cols(i)], q_recv.at[i], load_sem.at[3]),
        pltpu.make_async_copy(skip_hbm, skip_ref, load_sem.at[4]),
        pltpu.make_async_copy(section_hbm, section_ref, load_sem.at[5]),
        pltpu.make_async_copy(twist_hbm, twist_ref, load_sem.at[6]),
        pltpu.make_async_copy(forth_hbm, forth_ref, load_sem.at[7]),
        pltpu.make_async_copy(inverse_hbm, inverse_ref, load_sem.at[8]),
        pltpu.make_async_copy(back_hbm, back_ref, load_sem.at[9]),
        pltpu.make_async_copy(w_hbm, w_buf, load_sem.at[10]),
    ]
    for load in loads:
        load.start()
    pl.semaphore_wait(barrier, inner_n + outer_n + chan_n - 3)
    for r in range(1, outer_n):
        pl.semaphore_signal(ready, inc=1, device_id={"outer": at_outer(r)}, device_id_type=MESH)
    for load in loads[:4]:
        load.wait()

    def pack(index):
        span = cols(index)
        product = (k_buf[:, span].astype(F32) * v_buf[:, span].astype(F32)).astype(BF16)
        both = jnp.concatenate([product, taps_buf[:, span]], axis=1)
        rows = lax.dot_general(pick_ref[...], both, (((1,), (1,)), ((), ())), preferred_element_type=F32)
        return rows.reshape(outer_n, 2 * per, tok).astype(BF16)

    def d_copy(slot, r):
        there = order.index((inner_n - order[slot]) % inner_n)
        return pltpu.make_async_remote_copy(
            src_ref=send1.at[slot, at_outer(r)], dst_ref=recv2.at[o, there],
            send_sem=d_send.at[slot], recv_sem=d_recv.at[there],
            device_id={"outer": at_outer(r), "inner": at_inner(order[slot])}, device_id_type=MESH,
        )

    def d_all(slot):
        held = recv2.at[pl.ds(0, outer_n - 1 if slot == 0 else outer_n), slot]
        return pltpu.make_async_remote_copy(
            src_ref=held, dst_ref=held, send_sem=d_send.at[slot], recv_sem=d_recv.at[slot],
            device_id={"outer": sibling}, device_id_type=MESH,
        )

    def d_start(slot, first):
        def start(r, carry):
            d_copy(slot, r).start()
            return carry

        lax.fori_loop(first, outer_n, start, 0)

    for slot in range(inner_n):
        send1[slot] = pack(at_inner(order[slot]))
        if slot == 0:
            d_start(0, 1)
        else:
            d_copy(slot, 0).start()
    pl.semaphore_wait(ready, outer_n - 1)
    for slot in range(1, inner_n):
        d_start(slot, 1)
    recv2[o, 0] = send1[0, o]

    def q_copy(d):
        return pltpu.make_async_remote_copy(
            src_ref=q_hbm.at[:, cols(at_inner(d))], dst_ref=q_recv.at[i],
            send_sem=q_send.at[d], recv_sem=q_recv_sem.at[inner_n - d],
            device_id={"inner": at_inner(d)}, device_id_type=MESH,
        )

    for load in loads[4:]:
        load.wait()
    mine = pl.ds(core * (parts // 2), parts // 2)
    spans = w_rows.shape[0]

    def span_of(n):
        return pl.ds(n * w_rows.shape[2], w_rows.shape[2])

    def w_copy(d, n):
        held = weights.at[c, mine, span_of(n)]
        return pltpu.make_async_remote_copy(
            src_ref=held, dst_ref=held, send_sem=w_send.at[d, n], recv_sem=w_recv.at[chan_n - d, n],
            device_id={"chan": at_chan(d)}, device_id_type=MESH,
        )

    def f_copy(d, half):
        held = weights.at[at_chan(d), pl.ds(half * (parts // 2), parts // 2)]
        return pltpu.make_async_remote_copy(
            src_ref=held, dst_ref=held, send_sem=f_send.at[d], recv_sem=f_recv.at[d],
            device_id={"outer": sibling}, device_id_type=MESH,
        )

    def w_part(n):
        w_rows[n] = w_buf[:, span_of(n)].astype(F32)
        for cc in range(per):
            rows = w_rows[n, pl.ds(cc, slabs, stride=per), :]
            weights[c, cc // each, span_of(n), pl.ds(cc % each * slabs, slabs)] = rows.T.astype(BF16)
        for d in range(1, chan_n):
            w_copy(d, n).start()

    for n in range(spans):
        w_part(n)
    gains[...] = jnp.broadcast_to(skip_ref[:, cols(i)], (tok, block)).T

    def q_start():
        for d in order[1:]:
            q_copy(d).start()

    for slot in range(inner_n):
        if slot == Q_AT:
            q_start()
        d_all(slot).wait_recv()
        place = at_inner(order[slot])
        for source in range(outer_n):
            row = pl.multiple_of((source * inner_n + place) * (2 * per), 2 * per)
            signals[pl.ds(row, 2 * per), :] = recv2[source, slot].astype(F32)
    if Q_AT >= inner_n:
        q_start()

    padded = twist_ref.shape[1]
    cos_twist, sin_twist = twist_ref[0], twist_ref[1]
    own_gains = gains[pl.ds(pl.multiple_of(o * per, per), per), :]

    def wide(table, times):
        return jnp.concatenate([table] * times, axis=1)

    def convolve(first):
        both = [
            signals[pl.ds(channel + kind * per, slabs, stride=2 * per), :]
            for channel in (first, first + 1)
            for kind in range(2)
        ]
        x = jnp.concatenate([b.astype(BF16) for b in both], axis=1)
        y = dot(section_ref[...], jnp.concatenate([x, x], axis=0))
        real, imag = y[:padded], y[padded:]
        cos4, sin4 = wide(cos_twist, 4), wide(sin_twist, 4)
        turned_real = real * cos4 + imag * sin4
        turned_imag = imag * cos4 - real * sin4
        stacked = jnp.concatenate(
            [
                jnp.concatenate([t[:, n * tok : (n + 1) * tok] for t in (turned_real, turned_imag)], axis=1)
                for n in range(4)
            ],
            axis=0,
        )
        spec = dot3(stacked, forth_ref)
        prods = []
        for n in range(2):
            a = spec[2 * n * padded : (2 * n + 1) * padded]
            b = spec[(2 * n + 1) * padded : (2 * n + 2) * padded]
            ar, ai, br, bi = a[:, :tok], a[:, tok:], b[:, :tok], b[:, tok:]
            prods.append(jnp.concatenate([ar * br - ai * bi, ar * bi + ai * br], axis=1))
        ret = dot3(jnp.concatenate(prods, axis=0), inverse_ref)
        ups = []
        for n in range(2):
            r = ret[n * padded : (n + 1) * padded]
            rr, ri = r[:, :tok], r[:, tok:]
            ups.append(
                jnp.concatenate([rr * cos_twist - ri * sin_twist, ri * cos_twist + rr * sin_twist], axis=0)
            )
        high, low = halves(jnp.concatenate(ups, axis=1))
        conv = dot(back_ref[0], high) + (dot(back_ref[1], high) + dot(back_ref[0], low))
        mixed = [
            conv[:, n * tok : (n + 1) * tok] + own_gains[first + n : first + n + 1] * both[2 * n] for n in range(2)
        ]
        return jnp.concatenate([m.reshape(outer_n, inner_n, tok) for m in mixed], axis=1).astype(BF16)

    def part_rows(h):
        return pl.ds(h * each * inner_n, each * inner_n)

    def b_copy(h, r):
        return pltpu.make_async_remote_copy(
            src_ref=send2.at[at_outer(r), part_rows(h)], dst_ref=recv3.at[o, part_rows(h)],
            send_sem=b_send.at[h, r], recv_sem=b_recv.at[h, outer_n - r],
            device_id={"outer": at_outer(r)}, device_id_type=MESH,
        )

    def b_arrival(h, r):
        here = recv3.at[at_outer(r), part_rows(h)]
        return pltpu.make_async_remote_copy(
            src_ref=here, dst_ref=here, send_sem=b_send.at[h, r], recv_sem=b_recv.at[h, r],
            device_id={"outer": at_outer(r)}, device_id_type=MESH,
        )

    for h in range(parts):
        for pair in range(h * each // 2, (h + 1) * each // 2):
            send2[:, pl.ds(pair * 2 * inner_n, 2 * inner_n), :] = convolve(2 * pair)

        def b_start(r, carry, h=h):
            b_copy(h, r).start()
            return carry

        lax.fori_loop(1, outer_n, b_start, 0)
    recv3[o] = send2[o]

    for d in range(1, inner_n):
        q_copy(inner_n - d).wait_recv()
    for slab in range(inner_n):
        folded[pl.ds(slab * block, block), :] = q_recv[slab].astype(F32).T
        for cc in range(per):
            gate_q[cc, slab] = folded[pl.ds(slab * block + cc, outer_n, stride=per), :]

    def x_copy(h, d):
        return pltpu.make_async_remote_copy(
            src_ref=gx.at[h, at_chan(d)], dst_ref=gated.at[h, c, :, i],
            send_sem=x_send.at[h, d], recv_sem=x_recv.at[h, chan_n - d],
            device_id={"chan": at_chan(d)}, device_id_type=MESH,
        )

    for h in range(parts):

        def b_wait(r, carry, h=h):
            b_arrival(h, r).wait_recv()
            return carry

        lax.fori_loop(1, outer_n, b_wait, 0)
        count = each * inner_n
        first = h * outer_n * count
        for source in range(outer_n):
            conv_rows[pl.ds(first + source * count, count), :] = recv3[source, part_rows(h), :].astype(F32)
        for e in range(each):
            cc = h * each + e
            for slab in range(inner_n):
                conv = conv_rows[pl.ds(first + e * inner_n + slab, outer_n, stride=count), :]
                value = (gate_q[cc, slab] * conv).astype(BF16)
                gx[h, slab // near, e, :, pl.ds(slab % near * tok, tok)] = value
        for d in range(1, chan_n):
            x_copy(h, d).start()
        gated[h, c, :, i] = gx[h, c]

    longest = inner_n // 2

    def reach(way, h):
        return longest if (h + way) % 2 == 0 else inner_n - 1 - longest

    def g_copy(way, h, r, arrival=False):
        step = 1 if way == 0 else inner_n - 1
        source = at_inner((inner_n - step) * (r if arrival else r - 1) % inner_n)
        held = gated.at[h, :, :, source]
        return pltpu.make_async_remote_copy(
            src_ref=held, dst_ref=held,
            send_sem=g_send.at[way, h, r - 1], recv_sem=g_recv.at[way, h, r - 1],
            device_id={"inner": at_inner(step)}, device_id_type=MESH,
        )

    events = []
    for h in range(parts):
        for r in range(1, longest + 2):
            events.append((RING_LAG * h + r, h, r))
    for count, (_, h, r) in enumerate(sorted(events)):
        if count == PASS_AT:
            for d in range(1, chan_n):
                for n in range(spans):
                    w_copy(chan_n - d, n).wait_recv()
                f_copy(d, core).start()
        if r == 1:
            for d in range(1, chan_n):
                x_copy(h, chan_n - d).wait_recv()
        for way in range(2):
            if 1 < r <= reach(way, h) + 1:
                g_copy(way, h, r - 1, arrival=True).wait_recv()
            if r <= reach(way, h):
                g_copy(way, h, r).start()
        if r == longest + 1:
            if h == 0:
                for d in range(1, chan_n):
                    f_copy(d, 1 - core).wait_recv()
            part = None
            for group in range(chan_n):
                left, right = weights[group, h], gated[h, group].reshape(each * slabs, near * tok)
                term = dot(left, right)
                part = term if part is None else part + term
            if h < parts - 1:
                total[...] = part if h == 0 else total[...] + part
            else:
                out_ref[...] = (total[...] + part).T.astype(BF16)

    for slot in range(inner_n):
        d_all(slot).wait_send()
    for d in range(1, inner_n):
        q_copy(d).wait_send()

    def sent(r, carry):
        for h in range(parts):
            b_copy(h, r).wait_send()
        return carry

    lax.fori_loop(1, outer_n, sent, 0)
    for d in range(1, chan_n):
        for n in range(spans):
            w_copy(d, n).wait_send()
        f_copy(d, core).wait_send()
        for h in range(parts):
            x_copy(h, d).wait_send()
    for h in range(parts):
        for way in range(2):
            for r in range(1, reach(way, h) + 1):
                g_copy(way, h, r).wait_send()


def local(q_stream, k_stream, v_stream, filter_taps, skip_gain, out_weight):
    tok, chans = k_stream.shape
    outer_n, inner_n, chan_n = (lax.axis_size(a) for a in ("outer", "inner", "chan"))
    slabs = outer_n * inner_n
    per = chans // slabs
    block = outer_n * per
    width = out_weight.shape[1]
    coarse = inner_n * tok
    piece = coarse // chan_n
    held = (*tables(slabs, tok), pick_table(outer_n, per))
    parts = PARTS
    each = per // parts
    lanes = min(width, 128)
    sizes = (outer_n, inner_n, chan_n, tok, per, parts)
    spans = width // lanes
    dma = pltpu.SemaphoreType.DMA
    hbm = pl.BlockSpec(memory_space=pltpu.HBM)
    return pl.pallas_call(
        functools.partial(kernel, sizes),
        out_shape=jax.ShapeDtypeStruct((piece, width), BF16),
        in_specs=[hbm] * 12,
        out_specs=pl.BlockSpec(memory_space=pltpu.VMEM),
        scratch_shapes=[
            pltpu.VMEM((tok, chans), BF16),
            pltpu.VMEM((tok, chans), BF16),
            pltpu.VMEM((tok, chans), BF16),
            pltpu.VMEM((1, chans), F32),
            pltpu.VMEM((chans, width), BF16),
            *(pltpu.VMEM(t.shape, t.dtype) for t in held),
            pltpu.VMEM((inner_n, outer_n, 2 * per, tok), BF16),
            pltpu.VMEM((outer_n, inner_n, 2 * per, tok), BF16),
            pltpu.VMEM((slabs * 2 * per, tok), F32),
            pltpu.VMEM((outer_n, per * inner_n, tok), BF16),
            pltpu.VMEM((outer_n, per * inner_n, tok), BF16),
            pltpu.VMEM((outer_n * per * inner_n, tok), F32),
            pltpu.VMEM((inner_n, tok, block), BF16),
            pltpu.VMEM((block, tok), F32),
            pltpu.VMEM((inner_n * block, tok), F32),
            pltpu.VMEM((per, inner_n, outer_n, tok), F32),
            pltpu.VMEM((parts, chan_n, each, outer_n, piece), BF16),
            pltpu.VMEM((parts, chan_n, each, inner_n, outer_n, piece), BF16),
            pltpu.VMEM((width // lanes, chans, lanes), F32),
            pltpu.VMEM((chan_n, parts, width, each * slabs), BF16),
            pltpu.VMEM((width, piece), F32),
            dma((12,)),
            pltpu.SemaphoreType.REGULAR,
            dma((inner_n,)),
            dma((inner_n,)),
            dma((inner_n,)),
            dma((inner_n,)),
            dma((parts, outer_n)),
            dma((parts, outer_n)),
            dma((parts, chan_n)),
            dma((parts, chan_n)),
            dma((2, parts, inner_n // 2)),
            dma((2, parts, inner_n // 2)),
            dma((chan_n, spans)),
            dma((chan_n, spans)),
            dma((chan_n,)),
            dma((chan_n,)),
        ],
        compiler_params=pltpu.CompilerParams(
            collective_id=0, has_side_effects=True, vmem_limit_bytes=60 * 1024 * 1024
        ),
    )(q_stream, k_stream, v_stream, filter_taps, skip_gain[None, :], out_weight, *(jnp.asarray(t) for t in held))


def solution(mesh):
    return jax.shard_map(
        local,
        mesh=mesh,
        in_specs=(
            P(("outer", "inner"), "chan"),
            P(("outer", "inner"), "chan"),
            P(("outer", "inner"), "chan"),
            P(("outer", "inner"), "chan"),
            P("chan"),
            P("chan", "inner"),
        ),
        out_specs=P(("outer", "chan"), "inner"),
        check_vma=False,
    )
```

```python
import functools

import jax
import jax.numpy as jnp
import numpy as np
from jax import lax
from jax.experimental import pallas as pl
from jax.experimental.pallas import tpu as pltpu
from jax.sharding import PartitionSpec as P

MESH = pl.DeviceIdType.MESH
F32 = jnp.float32
BF16 = jnp.bfloat16
PARTS = 4
RING_LAG = 0.3
Q_AT = 1
PASS_AT = 3


def split_table(values):
    high = values.astype(np.float32).astype(jnp.bfloat16)
    low = (values - high.astype(np.float64)).astype(np.float32).astype(jnp.bfloat16)
    return high, low


@functools.lru_cache(maxsize=None)
def tables(slabs, tok):
    coarse = 2 * slabs
    total = coarse * tok
    rows = slabs + 1
    padded = -(-rows // 16) * 16
    k = np.arange(padded)
    live = (k < rows).astype(np.float64)
    angle = 2 * np.pi * ((k[:, None] * np.arange(slabs)[None, :]) % coarse) / coarse
    cos, sin = np.cos(angle) * live[:, None], np.sin(angle) * live[:, None]
    section = np.concatenate(split_table(np.concatenate([cos, -sin], axis=0)), axis=1)
    weight = np.where((k == 0) | (k == slabs), 1.0, 2.0) / total
    back = np.concatenate([(cos * weight[:, None]).T, (-sin * weight[:, None]).T], axis=1)
    back = np.stack(split_table(back))
    turn = 2 * np.pi * ((k[:, None] * np.arange(tok)[None, :]) % total) / total
    twist = np.stack([np.cos(turn), np.sin(turn)]).astype(np.float32)
    m = np.arange(tok)
    fine = 2 * np.pi * ((m[:, None] * m[None, :]) % tok) / tok
    c, s = np.cos(fine), np.sin(fine)
    forth = np.stack(split_table(np.block([[c, -s], [s, c]])))
    inverse = np.stack(split_table(np.block([[c, s], [-s, c]])))
    return section, twist, forth, inverse, back


def pick_table(outer_n, per):
    block = outer_n * per
    device, signal, channel = np.meshgrid(np.arange(outer_n), np.arange(2), np.arange(per), indexing="ij")
    column = (signal * block + device * per + channel).reshape(-1)
    return (column[:, None] == np.arange(2 * block)[None, :]).astype(np.float32).astype(jnp.bfloat16)


def dot(a, b):
    return jnp.dot(a, b, preferred_element_type=F32)


def halves(x):
    high = x.astype(BF16)
    return high, (x - high.astype(F32)).astype(BF16)


def dot3(x, table):
    high, low = halves(x)
    return dot(high, table[0]) + (dot(high, table[1]) + dot(low, table[0]))


def near_first(n):
    order = [0]
    for d in range(1, n // 2):
        order += [d, n - d]
    return order + [n // 2]


def kernel(
    sizes,
    q_hbm, k_hbm, v_hbm, taps_hbm, skip_hbm, w_hbm,
    section_hbm, twist_hbm, forth_hbm, inverse_hbm, back_hbm, pick_hbm,
    out_ref,
    k_buf, v_buf, taps_buf, skip_ref, w_buf, section_ref, twist_ref, forth_ref, inverse_ref, back_ref, pick_ref,
    send1, recv1, recv2, signals, send2, recv3, conv_rows, q_recv, gains, folded, gate_q,
    gx, gated, w_rows, weights, total,
    load_sem, ready, y_send, y_recv, z_send, z_recv, d_send, d_recv, q_send, q_recv_sem, b_send, b_recv, x_send, x_recv,
    g_send, g_recv, w_send, w_recv, f_send, f_recv,
):
    outer_n, inner_n, chan_n, tok, per, parts = sizes
    slabs = outer_n * inner_n
    block = outer_n * per
    each = per // parts
    o, i, c = lax.axis_index("outer"), lax.axis_index("inner"), lax.axis_index("chan")
    order = near_first(inner_n)
    near = inner_n // chan_n
    passed = inner_n // 2
    waves = [(low, low + 2) for low in range(1, passed + 1, 2)]
    core = lax.rem(o, 2)
    sibling = o + 1 - 2 * core

    def at_inner(d):
        return lax.rem(i + d, inner_n)

    def at_outer(r):
        return lax.rem(o + r, outer_n)

    def at_chan(d):
        return lax.rem(c + d, chan_n)

    def cols(index):
        return pl.ds(pl.multiple_of(index * block, block), block)

    barrier = pltpu.get_barrier_semaphore()
    for d in range(1, inner_n):
        pl.semaphore_signal(barrier, inc=1, device_id={"inner": at_inner(d)}, device_id_type=MESH)
    for r in range(1, outer_n):
        pl.semaphore_signal(barrier, inc=1, device_id={"outer": at_outer(r)}, device_id_type=MESH)
    for d in range(1, chan_n):
        pl.semaphore_signal(barrier, inc=1, device_id={"chan": at_chan(d)}, device_id_type=MESH)

    loads = [
        pltpu.make_async_copy(k_hbm, k_buf, load_sem.at[0]),
        pltpu.make_async_copy(v_hbm, v_buf, load_sem.at[1]),
        pltpu.make_async_copy(taps_hbm, taps_buf, load_sem.at[2]),
        pltpu.make_async_copy(pick_hbm, pick_ref, load_sem.at[11]),
        pltpu.make_async_copy(q_hbm.at[:, cols(i)], q_recv.at[i], load_sem.at[3]),
        pltpu.make_async_copy(skip_hbm, skip_ref, load_sem.at[4]),
        pltpu.make_async_copy(section_hbm, section_ref, load_sem.at[5]),
        pltpu.make_async_copy(twist_hbm, twist_ref, load_sem.at[6]),
        pltpu.make_async_copy(forth_hbm, forth_ref, load_sem.at[7]),
        pltpu.make_async_copy(inverse_hbm, inverse_ref, load_sem.at[8]),
        pltpu.make_async_copy(back_hbm, back_ref, load_sem.at[9]),
        pltpu.make_async_copy(w_hbm, w_buf, load_sem.at[10]),
    ]
    for load in loads:
        load.start()
    pl.semaphore_wait(barrier, inner_n + outer_n + chan_n - 3)
    for r in range(1, outer_n):
        pl.semaphore_signal(ready, inc=1, device_id={"outer": at_outer(r)}, device_id_type=MESH)
    for load in loads[:4]:
        load.wait()

    def pack(index):
        span = cols(index)
        product = (k_buf[:, span].astype(F32) * v_buf[:, span].astype(F32)).astype(BF16)
        both = jnp.concatenate([product, taps_buf[:, span]], axis=1)
        rows = lax.dot_general(pick_ref[...], both, (((1,), (1,)), ((), ())), preferred_element_type=F32)
        return rows.reshape(outer_n, 2 * per, tok).astype(BF16)

    def d_copy(slot, r):
        there = order.index((inner_n - order[slot]) % inner_n)
        return pltpu.make_async_remote_copy(
            src_ref=send1.at[slot, at_outer(r)], dst_ref=recv2.at[o, there],
            send_sem=d_send.at[slot], recv_sem=d_recv.at[there],
            device_id={"outer": at_outer(r), "inner": at_inner(order[slot])}, device_id_type=MESH,
        )

    def d_all(slot):
        held = recv2.at[pl.ds(0, outer_n - 1 if slot == 0 else outer_n), slot]
        return pltpu.make_async_remote_copy(
            src_ref=held, dst_ref=held, send_sem=d_send.at[slot], recv_sem=d_recv.at[slot],
            device_id={"outer": sibling}, device_id_type=MESH,
        )

    def y_copy(slot, d):
        there = order.index((inner_n - d) % inner_n)
        return pltpu.make_async_remote_copy(
            src_ref=send1.at[slot], dst_ref=recv1.at[there - 1], send_sem=y_send.at[slot], recv_sem=y_recv.at[there],
            device_id={"inner": at_inner(d)}, device_id_type=MESH,
        )

    def z_copy(wave, r):
        low, high = waves[wave]
        return pltpu.make_async_remote_copy(
            src_ref=recv1.at[pl.ds(low - 1, high - low), at_outer(r)],
            dst_ref=recv2.at[o, pl.ds(low, high - low)],
            send_sem=z_send.at[wave], recv_sem=z_recv.at[wave],
            device_id={"outer": at_outer(r)}, device_id_type=MESH,
        )

    def z_all(wave):
        low, high = waves[wave]
        held = recv2.at[pl.ds(0, outer_n - 1), pl.ds(low, high - low)]
        return pltpu.make_async_remote_copy(
            src_ref=held, dst_ref=held, send_sem=z_send.at[wave], recv_sem=z_recv.at[wave],
            device_id={"outer": sibling}, device_id_type=MESH,
        )

    def d_start(slot, first):
        def start(r, carry):
            d_copy(slot, r).start()
            return carry

        lax.fori_loop(first, outer_n, start, 0)

    def q_copy(d):
        return pltpu.make_async_remote_copy(
            src_ref=q_hbm.at[:, cols(at_inner(d))], dst_ref=q_recv.at[i],
            send_sem=q_send.at[d], recv_sem=q_recv_sem.at[inner_n - d],
            device_id={"inner": at_inner(d)}, device_id_type=MESH,
        )

    def q_start():
        for d in order[1:]:
            q_copy(d).start()

    for slot in range(1, passed + 1):
        send1[slot] = pack(at_inner(order[slot]))
        y_copy(slot, order[slot]).start()
    send1[0] = pack(i)
    d_start(0, 1)
    recv2[o, 0] = send1[0, o]
    for slot in range(passed + 1, inner_n):
        send1[slot] = pack(at_inner(order[slot]))
    for load in loads[4:]:
        load.wait()
    mine = pl.ds(core * (parts // 2), parts // 2)
    spans = w_rows.shape[0]

    def span_of(n):
        return pl.ds(n * w_rows.shape[2], w_rows.shape[2])

    def w_copy(d, n):
        return pltpu.make_async_remote_copy(
            src_ref=weights.at[0, mine, span_of(n)], dst_ref=weights.at[chan_n - d, mine, span_of(n)],
            send_sem=w_send.at[d, n], recv_sem=w_recv.at[chan_n - d, n],
            device_id={"chan": at_chan(d)}, device_id_type=MESH,
        )

    def f_copy(d, half):
        held = weights.at[d, pl.ds(half * (parts // 2), parts // 2)]
        return pltpu.make_async_remote_copy(
            src_ref=held, dst_ref=held, send_sem=f_send.at[d], recv_sem=f_recv.at[d],
            device_id={"outer": sibling}, device_id_type=MESH,
        )

    def w_part(n):
        w_rows[n] = w_buf[:, span_of(n)].astype(F32)
        for cc in range(per):
            rows = w_rows[n, pl.ds(cc, slabs, stride=per), :]
            weights[0, cc // each, span_of(n), pl.ds(cc % each * slabs, slabs)] = rows.T.astype(BF16)
        for d in range(1, chan_n):
            w_copy(d, n).start()

    for n in range(spans):
        w_part(n)
    gains[...] = jnp.broadcast_to(skip_ref[:, cols(i)], (tok, block)).T

    if Q_AT == 0:
        q_start()
    pl.semaphore_wait(ready, outer_n - 1)
    for slot in range(passed + 1, inner_n):
        d_start(slot, 0)

    for wave, (low, high) in enumerate(waves):
        for slot in range(low, high):
            y_copy(slot, (inner_n - order[slot]) % inner_n).wait_recv()

        def z_start(r, carry, wave=wave):
            z_copy(wave, r).start()
            return carry

        lax.fori_loop(1, outer_n, z_start, 0)
        for slot in range(low, high):
            recv2[o, slot] = recv1[slot - 1, o]
    if Q_AT == 1:
        q_start()
    def spread(slot):
        place = at_inner(order[slot])
        for source in range(outer_n):
            row = pl.multiple_of((source * inner_n + place) * (2 * per), 2 * per)
            signals[pl.ds(row, 2 * per), :] = recv2[source, slot].astype(F32)

    for slot in [0, *range(passed + 1, inner_n)]:
        d_all(slot).wait_recv()
        spread(slot)
    if Q_AT == 2:
        q_start()
    for wave, (low, high) in enumerate(waves):
        z_all(wave).wait_recv()
        for slot in range(low, high):
            spread(slot)

    padded = twist_ref.shape[1]
    cos_twist, sin_twist = twist_ref[0], twist_ref[1]
    own_gains = gains[pl.ds(pl.multiple_of(o * per, per), per), :]

    def wide(table, times):
        return jnp.concatenate([table] * times, axis=1)

    def convolve(first):
        both = [
            signals[pl.ds(channel + kind * per, slabs, stride=2 * per), :]
            for channel in (first, first + 1)
            for kind in range(2)
        ]
        x = jnp.concatenate([b.astype(BF16) for b in both], axis=1)
        y = dot(section_ref[...], jnp.concatenate([x, x], axis=0))
        real, imag = y[:padded], y[padded:]
        cos4, sin4 = wide(cos_twist, 4), wide(sin_twist, 4)
        turned_real = real * cos4 + imag * sin4
        turned_imag = imag * cos4 - real * sin4
        stacked = jnp.concatenate(
            [
                jnp.concatenate([t[:, n * tok : (n + 1) * tok] for t in (turned_real, turned_imag)], axis=1)
                for n in range(4)
            ],
            axis=0,
        )
        spec = dot3(stacked, forth_ref)
        prods = []
        for n in range(2):
            a = spec[2 * n * padded : (2 * n + 1) * padded]
            b = spec[(2 * n + 1) * padded : (2 * n + 2) * padded]
            ar, ai, br, bi = a[:, :tok], a[:, tok:], b[:, :tok], b[:, tok:]
            prods.append(jnp.concatenate([ar * br - ai * bi, ar * bi + ai * br], axis=1))
        ret = dot3(jnp.concatenate(prods, axis=0), inverse_ref)
        ups = []
        for n in range(2):
            r = ret[n * padded : (n + 1) * padded]
            rr, ri = r[:, :tok], r[:, tok:]
            ups.append(
                jnp.concatenate([rr * cos_twist - ri * sin_twist, ri * cos_twist + rr * sin_twist], axis=0)
            )
        high, low = halves(jnp.concatenate(ups, axis=1))
        conv = dot(back_ref[0], high) + (dot(back_ref[1], high) + dot(back_ref[0], low))
        mixed = [
            conv[:, n * tok : (n + 1) * tok] + own_gains[first + n : first + n + 1] * both[2 * n] for n in range(2)
        ]
        return jnp.concatenate([m.reshape(outer_n, inner_n, tok) for m in mixed], axis=1).astype(BF16)

    def part_rows(h):
        return pl.ds(h * each * inner_n, each * inner_n)

    def b_copy(h, r):
        return pltpu.make_async_remote_copy(
            src_ref=send2.at[at_outer(r), part_rows(h)], dst_ref=recv3.at[o, part_rows(h)],
            send_sem=b_send.at[h, r], recv_sem=b_recv.at[h, outer_n - r],
            device_id={"outer": at_outer(r)}, device_id_type=MESH,
        )

    def b_arrival(h, r):
        here = recv3.at[at_outer(r), part_rows(h)]
        return pltpu.make_async_remote_copy(
            src_ref=here, dst_ref=here, send_sem=b_send.at[h, r], recv_sem=b_recv.at[h, r],
            device_id={"outer": at_outer(r)}, device_id_type=MESH,
        )

    for h in range(parts):
        for pair in range(h * each // 2, (h + 1) * each // 2):
            send2[:, pl.ds(pair * 2 * inner_n, 2 * inner_n), :] = convolve(2 * pair)

        def b_start(r, carry, h=h):
            b_copy(h, r).start()
            return carry

        lax.fori_loop(1, outer_n, b_start, 0)
    recv3[o] = send2[o]

    for d in range(1, inner_n):
        q_copy(inner_n - d).wait_recv()
    for slab in range(inner_n):
        folded[pl.ds(slab * block, block), :] = q_recv[slab].astype(F32).T
        for cc in range(per):
            gate_q[cc, slab] = folded[pl.ds(slab * block + cc, outer_n, stride=per), :]

    def x_copy(h, d):
        return pltpu.make_async_remote_copy(
            src_ref=gx.at[h, at_chan(d)], dst_ref=gated.at[h, chan_n - d, :, i],
            send_sem=x_send.at[h, d], recv_sem=x_recv.at[h, chan_n - d],
            device_id={"chan": at_chan(d)}, device_id_type=MESH,
        )

    longest = inner_n // 2
    OWN, REST, WHOLE = 0, 1, 2

    def reach(way, h):
        return longest if (h + way) % 2 == 0 else inner_n - 1 - longest

    def g_copy(way, h, r, which, arrival=False):
        step = 1 if way == 0 else inner_n - 1
        source = at_inner((inner_n - step) * (r if arrival else r - 1) % inner_n)
        groups = (pl.ds(0, 1), pl.ds(1, chan_n - 1), pl.ds(0, chan_n))[which]
        held = gated.at[h, groups, :, source]
        place = 0 if which == OWN else r
        return pltpu.make_async_remote_copy(
            src_ref=held, dst_ref=held,
            send_sem=g_send.at[way, h, place], recv_sem=g_recv.at[way, h, place],
            device_id={"inner": at_inner(step)}, device_id_type=MESH,
        )

    for h in range(parts):

        def b_wait(r, carry, h=h):
            b_arrival(h, r).wait_recv()
            return carry

        lax.fori_loop(1, outer_n, b_wait, 0)
        count = each * inner_n
        first = h * outer_n * count
        for source in range(outer_n):
            conv_rows[pl.ds(first + source * count, count), :] = recv3[source, part_rows(h), :].astype(F32)
        for e in range(each):
            cc = h * each + e
            for slab in range(inner_n):
                conv = conv_rows[pl.ds(first + e * inner_n + slab, outer_n, stride=count), :]
                value = (gate_q[cc, slab] * conv).astype(BF16)
                gx[h, slab // near, e, :, pl.ds(slab % near * tok, tok)] = value
        for d in range(1, chan_n):
            x_copy(h, d).start()
        gated[h, 0, :, i] = gx[h, c]
        for way in range(2):
            g_copy(way, h, 1, OWN).start()

    events = []
    for h in range(parts):
        for r in range(1, longest + 2):
            events.append((RING_LAG * h + r, h, r))
    for count, (_, h, r) in enumerate(sorted(events)):
        if count == PASS_AT:
            for d in range(1, chan_n):
                for n in range(spans):
                    w_copy(chan_n - d, n).wait_recv()
                f_copy(d, core).start()
        if r == 1:
            for d in range(1, chan_n):
                x_copy(h, chan_n - d).wait_recv()
        for way in range(2):
            if r == 2:
                g_copy(way, h, 1, OWN, arrival=True).wait_recv()
            if 1 < r <= reach(way, h) + 1:
                g_copy(way, h, r - 1, REST if r == 2 else WHOLE, arrival=True).wait_recv()
            if r <= reach(way, h):
                g_copy(way, h, r, REST if r == 1 else WHOLE).start()
        if r == longest + 1:
            if h == 0:
                for d in range(1, chan_n):
                    f_copy(d, 1 - core).wait_recv()
            part = None
            for group in range(chan_n):
                left, right = weights[group, h], gated[h, group].reshape(each * slabs, near * tok)
                term = dot(left, right)
                part = term if part is None else part + term
            if h < parts - 1:
                total[...] = part if h == 0 else total[...] + part
            else:
                out_ref[...] = (total[...] + part).T.astype(BF16)

    for slot in [0, *range(passed + 1, inner_n)]:
        d_all(slot).wait_send()
    for slot in range(1, passed + 1):
        y_copy(slot, order[slot]).wait_send()
    for wave in range(len(waves)):
        z_all(wave).wait_send()
    for d in range(1, inner_n):
        q_copy(d).wait_send()

    def sent(r, carry):
        for h in range(parts):
            b_copy(h, r).wait_send()
        return carry

    lax.fori_loop(1, outer_n, sent, 0)
    for d in range(1, chan_n):
        for n in range(spans):
            w_copy(d, n).wait_send()
        f_copy(d, core).wait_send()
        for h in range(parts):
            x_copy(h, d).wait_send()
    for h in range(parts):
        for way in range(2):
            g_copy(way, h, 1, OWN).wait_send()
            for r in range(1, reach(way, h) + 1):
                g_copy(way, h, r, REST if r == 1 else WHOLE).wait_send()


def local(q_stream, k_stream, v_stream, filter_taps, skip_gain, out_weight):
    tok, chans = k_stream.shape
    outer_n, inner_n, chan_n = (lax.axis_size(a) for a in ("outer", "inner", "chan"))
    slabs = outer_n * inner_n
    per = chans // slabs
    block = outer_n * per
    width = out_weight.shape[1]
    coarse = inner_n * tok
    piece = coarse // chan_n
    held = (*tables(slabs, tok), pick_table(outer_n, per))
    parts = PARTS
    each = per // parts
    lanes = min(width, 128)
    sizes = (outer_n, inner_n, chan_n, tok, per, parts)
    spans = width // lanes
    dma = pltpu.SemaphoreType.DMA
    hbm = pl.BlockSpec(memory_space=pltpu.HBM)
    return pl.pallas_call(
        functools.partial(kernel, sizes),
        out_shape=jax.ShapeDtypeStruct((piece, width), BF16),
        in_specs=[hbm] * 12,
        out_specs=pl.BlockSpec(memory_space=pltpu.VMEM),
        scratch_shapes=[
            pltpu.VMEM((tok, chans), BF16),
            pltpu.VMEM((tok, chans), BF16),
            pltpu.VMEM((tok, chans), BF16),
            pltpu.VMEM((1, chans), F32),
            pltpu.VMEM((chans, width), BF16),
            *(pltpu.VMEM(t.shape, t.dtype) for t in held),
            pltpu.VMEM((inner_n, outer_n, 2 * per, tok), BF16),
            pltpu.VMEM((inner_n // 2, outer_n, 2 * per, tok), BF16),
            pltpu.VMEM((outer_n, inner_n, 2 * per, tok), BF16),
            pltpu.VMEM((slabs * 2 * per, tok), F32),
            pltpu.VMEM((outer_n, per * inner_n, tok), BF16),
            pltpu.VMEM((outer_n, per * inner_n, tok), BF16),
            pltpu.VMEM((outer_n * per * inner_n, tok), F32),
            pltpu.VMEM((inner_n, tok, block), BF16),
            pltpu.VMEM((block, tok), F32),
            pltpu.VMEM((inner_n * block, tok), F32),
            pltpu.VMEM((per, inner_n, outer_n, tok), F32),
            pltpu.VMEM((parts, chan_n, each, outer_n, piece), BF16),
            pltpu.VMEM((parts, chan_n, each, inner_n, outer_n, piece), BF16),
            pltpu.VMEM((width // lanes, chans, lanes), F32),
            pltpu.VMEM((chan_n, parts, width, each * slabs), BF16),
            pltpu.VMEM((width, piece), F32),
            dma((12,)),
            pltpu.SemaphoreType.REGULAR,
            dma((inner_n,)),
            dma((inner_n,)),
            dma((inner_n // 4,)),
            dma((inner_n // 4,)),
            dma((inner_n,)),
            dma((inner_n,)),
            dma((inner_n,)),
            dma((inner_n,)),
            dma((parts, outer_n)),
            dma((parts, outer_n)),
            dma((parts, chan_n)),
            dma((parts, chan_n)),
            dma((2, parts, inner_n // 2 + 1)),
            dma((2, parts, inner_n // 2 + 1)),
            dma((chan_n, spans)),
            dma((chan_n, spans)),
            dma((chan_n,)),
            dma((chan_n,)),
        ],
        compiler_params=pltpu.CompilerParams(
            collective_id=0, has_side_effects=True, vmem_limit_bytes=60 * 1024 * 1024
        ),
    )(q_stream, k_stream, v_stream, filter_taps, skip_gain[None, :], out_weight, *(jnp.asarray(t) for t in held))


def solution(mesh):
    return jax.shard_map(
        local,
        mesh=mesh,
        in_specs=(
            P(("outer", "inner"), "chan"),
            P(("outer", "inner"), "chan"),
            P(("outer", "inner"), "chan"),
            P(("outer", "inner"), "chan"),
            P("chan"),
            P("chan", "inner"),
        ),
        out_specs=P(("outer", "chan"), "inner"),
        check_vma=False,
    )
```

```python
import functools

import jax
import jax.numpy as jnp
import numpy as np
from jax import lax
from jax.experimental import pallas as pl
from jax.experimental.pallas import tpu as pltpu
from jax.sharding import PartitionSpec as P

MESH = pl.DeviceIdType.MESH
F32 = jnp.float32
BF16 = jnp.bfloat16
PARTS = 4
RING_LAG = 0.3
PASS_AT = 3


def split_table(values):
    high = values.astype(np.float32).astype(jnp.bfloat16)
    low = (values - high.astype(np.float64)).astype(np.float32).astype(jnp.bfloat16)
    return high, low


@functools.lru_cache(maxsize=None)
def tables(slabs, tok):
    coarse = 2 * slabs
    total = coarse * tok
    rows = slabs + 1
    padded = -(-rows // 16) * 16
    k = np.arange(padded)
    live = (k < rows).astype(np.float64)
    angle = 2 * np.pi * ((k[:, None] * np.arange(slabs)[None, :]) % coarse) / coarse
    cos, sin = np.cos(angle) * live[:, None], np.sin(angle) * live[:, None]
    section = np.concatenate(split_table(np.concatenate([cos, -sin], axis=0)), axis=1)
    weight = np.where((k == 0) | (k == slabs), 1.0, 2.0) / total
    back = np.concatenate([(cos * weight[:, None]).T, (-sin * weight[:, None]).T], axis=1)
    back = np.stack(split_table(back))
    turn = 2 * np.pi * ((k[:, None] * np.arange(tok)[None, :]) % total) / total
    twist = np.stack([np.cos(turn), np.sin(turn)]).astype(np.float32)
    m = np.arange(tok)
    fine = 2 * np.pi * ((m[:, None] * m[None, :]) % tok) / tok
    c, s = np.cos(fine), np.sin(fine)
    forth = np.stack(split_table(np.block([[c, -s], [s, c]])))
    inverse = np.stack(split_table(np.block([[c, s], [-s, c]])))
    return section, twist, forth, inverse, back


def pick_table(outer_n, per):
    block = outer_n * per
    device, signal, channel = np.meshgrid(np.arange(outer_n), np.arange(2), np.arange(per), indexing="ij")
    column = (signal * block + device * per + channel).reshape(-1)
    return (column[:, None] == np.arange(2 * block)[None, :]).astype(np.float32).astype(jnp.bfloat16)


def dot(a, b):
    return jnp.dot(a, b, preferred_element_type=F32)


def halves(x):
    high = x.astype(BF16)
    return high, (x - high.astype(F32)).astype(BF16)


def dot3(x, table):
    high, low = halves(x)
    return dot(high, table[0]) + (dot(high, table[1]) + dot(low, table[0]))


def path_order(n):
    order = [0]
    for d in range(1, n // 2 - 1):
        order += [d, n - d]
    return order + [n // 2, n // 2 - 1, n // 2 + 1]


def kernel(
    sizes,
    q_hbm, k_hbm, v_hbm, taps_hbm, skip_hbm, w_hbm,
    section_hbm, twist_hbm, forth_hbm, inverse_hbm, back_hbm, pick_hbm,
    out_ref,
    k_buf, v_buf, taps_buf, skip_ref, w_buf, section_ref, twist_ref, forth_ref, inverse_ref, back_ref, pick_ref,
    send1, recv1, middle, recv2, signals, send2, recv3, conv_rows, q_recv, gains, folded, gate_q,
    gx, gated, w_rows, weights, total,
    load_sem, y_send, y_recv, z_send, z_recv, t_send, t_recv, d_send, d_recv, q_send, q_recv_sem, b_send, b_recv, x_send, x_recv,
    g_send, g_recv, w_send, w_recv, f_send, f_recv,
):
    outer_n, inner_n, chan_n, tok, per, parts = sizes
    slabs = outer_n * inner_n
    block = outer_n * per
    each = per // parts
    o, i, c = lax.axis_index("outer"), lax.axis_index("inner"), lax.axis_index("chan")
    order = path_order(inner_n)
    near = inner_n // chan_n
    passed = inner_n - 3
    waves = [(low, min(low + 2, passed + 1)) for low in range(1, passed + 1, 2)]
    turned = (passed + 1, passed + 2)
    core = lax.rem(o, 2)
    sibling = o + 1 - 2 * core

    def at_inner(d):
        return lax.rem(i + d, inner_n)

    def at_outer(r):
        return lax.rem(o + r, outer_n)

    def at_chan(d):
        return lax.rem(c + d, chan_n)

    def cols(index):
        return pl.ds(pl.multiple_of(index * block, block), block)

    barrier = pltpu.get_barrier_semaphore()
    for d in range(1, inner_n):
        pl.semaphore_signal(barrier, inc=1, device_id={"inner": at_inner(d)}, device_id_type=MESH)
    for r in range(1, outer_n):
        pl.semaphore_signal(barrier, inc=1, device_id={"outer": at_outer(r)}, device_id_type=MESH)
    for d in range(1, chan_n):
        pl.semaphore_signal(barrier, inc=1, device_id={"chan": at_chan(d)}, device_id_type=MESH)

    loads = [
        pltpu.make_async_copy(k_hbm, k_buf, load_sem.at[0]),
        pltpu.make_async_copy(v_hbm, v_buf, load_sem.at[1]),
        pltpu.make_async_copy(taps_hbm, taps_buf, load_sem.at[2]),
        pltpu.make_async_copy(pick_hbm, pick_ref, load_sem.at[11]),
        pltpu.make_async_copy(q_hbm.at[:, cols(i)], q_recv.at[i], load_sem.at[3]),
        pltpu.make_async_copy(skip_hbm, skip_ref, load_sem.at[4]),
        pltpu.make_async_copy(section_hbm, section_ref, load_sem.at[5]),
        pltpu.make_async_copy(twist_hbm, twist_ref, load_sem.at[6]),
        pltpu.make_async_copy(forth_hbm, forth_ref, load_sem.at[7]),
        pltpu.make_async_copy(inverse_hbm, inverse_ref, load_sem.at[8]),
        pltpu.make_async_copy(back_hbm, back_ref, load_sem.at[9]),
        pltpu.make_async_copy(w_hbm, w_buf, load_sem.at[10]),
    ]
    for load in loads:
        load.start()
    pl.semaphore_wait(barrier, inner_n + outer_n + chan_n - 3)
    for load in loads[:4]:
        load.wait()

    def pack(index):
        span = cols(index)
        product = (k_buf[:, span].astype(F32) * v_buf[:, span].astype(F32)).astype(BF16)
        both = jnp.concatenate([product, taps_buf[:, span]], axis=1)
        rows = lax.dot_general(pick_ref[...], both, (((1,), (1,)), ((), ())), preferred_element_type=F32)
        return rows.reshape(outer_n, 2 * per, tok).astype(BF16)

    def d_copy(r):
        return pltpu.make_async_remote_copy(
            src_ref=send1.at[0, at_outer(r)], dst_ref=recv2.at[o, 0], send_sem=d_send.at[0], recv_sem=d_recv.at[0],
            device_id={"outer": at_outer(r)}, device_id_type=MESH,
        )

    def d_all():
        held = recv2.at[pl.ds(0, outer_n - 1), 0]
        return pltpu.make_async_remote_copy(
            src_ref=held, dst_ref=held, send_sem=d_send.at[0], recv_sem=d_recv.at[0],
            device_id={"outer": sibling}, device_id_type=MESH,
        )

    def t_copy(r):
        return pltpu.make_async_remote_copy(
            src_ref=send1.at[pl.ds(turned[0], 2), at_outer(r)], dst_ref=middle.at[:, o],
            send_sem=t_send.at[0], recv_sem=t_recv.at[0],
            device_id={"outer": at_outer(r)}, device_id_type=MESH,
        )

    def t_all():
        held = middle.at[:, pl.ds(0, outer_n - 1)]
        return pltpu.make_async_remote_copy(
            src_ref=held, dst_ref=held, send_sem=t_send.at[0], recv_sem=t_recv.at[0],
            device_id={"outer": sibling}, device_id_type=MESH,
        )

    def turn_copy(slot, d):
        there = order.index((inner_n - d) % inner_n)
        return pltpu.make_async_remote_copy(
            src_ref=middle.at[slot - turned[0]], dst_ref=recv2.at[:, there],
            send_sem=d_send.at[slot], recv_sem=d_recv.at[there],
            device_id={"inner": at_inner(d)}, device_id_type=MESH,
        )

    def y_copy(slot, d):
        there = order.index((inner_n - d) % inner_n)
        return pltpu.make_async_remote_copy(
            src_ref=send1.at[slot], dst_ref=recv1.at[there - 1], send_sem=y_send.at[slot], recv_sem=y_recv.at[there],
            device_id={"inner": at_inner(d)}, device_id_type=MESH,
        )

    def z_copy(wave, r):
        low, high = waves[wave]
        return pltpu.make_async_remote_copy(
            src_ref=recv1.at[pl.ds(low - 1, high - low), at_outer(r)],
            dst_ref=recv2.at[o, pl.ds(low, high - low)],
            send_sem=z_send.at[wave], recv_sem=z_recv.at[wave],
            device_id={"outer": at_outer(r)}, device_id_type=MESH,
        )

    def z_all(wave):
        low, high = waves[wave]
        held = recv2.at[pl.ds(0, outer_n - 1), pl.ds(low, high - low)]
        return pltpu.make_async_remote_copy(
            src_ref=held, dst_ref=held, send_sem=z_send.at[wave], recv_sem=z_recv.at[wave],
            device_id={"outer": sibling}, device_id_type=MESH,
        )

    def q_copy(d):
        return pltpu.make_async_remote_copy(
            src_ref=q_hbm.at[:, cols(at_inner(d))], dst_ref=q_recv.at[i],
            send_sem=q_send.at[d], recv_sem=q_recv_sem.at[inner_n - d],
            device_id={"inner": at_inner(d)}, device_id_type=MESH,
        )

    def q_start():
        for d in order[1:]:
            q_copy(d).start()

    def y_go(slot):
        send1[slot] = pack(at_inner(order[slot]))
        y_copy(slot, order[slot]).start()

    for slot in range(1, passed):
        y_go(slot)
    for slot in turned:
        send1[slot] = pack(at_inner(order[slot]))

    def t_start(r, carry):
        t_copy(r).start()
        return carry

    def d_start(r, carry):
        d_copy(r).start()
        return carry

    lax.fori_loop(1, outer_n, t_start, 0)
    middle[:, o] = send1[turned[0] : turned[1] + 1, o]
    send1[0] = pack(i)
    lax.fori_loop(1, outer_n, d_start, 0)
    recv2[o, 0] = send1[0, o]
    y_go(passed)

    for load in loads[4:]:
        load.wait()
    mine = pl.ds(core * (parts // 2), parts // 2)
    spans = w_rows.shape[0]

    def span_of(n):
        return pl.ds(n * w_rows.shape[2], w_rows.shape[2])

    def w_copy(d, n):
        return pltpu.make_async_remote_copy(
            src_ref=weights.at[0, mine, span_of(n)], dst_ref=weights.at[chan_n - d, mine, span_of(n)],
            send_sem=w_send.at[d, n], recv_sem=w_recv.at[chan_n - d, n],
            device_id={"chan": at_chan(d)}, device_id_type=MESH,
        )

    def f_copy(d, half):
        held = weights.at[d, pl.ds(half * (parts // 2), parts // 2)]
        return pltpu.make_async_remote_copy(
            src_ref=held, dst_ref=held, send_sem=f_send.at[d], recv_sem=f_recv.at[d],
            device_id={"outer": sibling}, device_id_type=MESH,
        )

    def w_part(n):
        w_rows[n] = w_buf[:, span_of(n)].astype(F32)
        for cc in range(per):
            rows = w_rows[n, pl.ds(cc, slabs, stride=per), :]
            weights[0, cc // each, span_of(n), pl.ds(cc % each * slabs, slabs)] = rows.T.astype(BF16)
        for d in range(1, chan_n):
            w_copy(d, n).start()

    for n in range(spans):
        w_part(n)
    gains[...] = jnp.broadcast_to(skip_ref[:, cols(i)], (tok, block)).T

    for wave, (low, high) in enumerate(waves):
        for slot in range(low, high):
            y_copy(slot, (inner_n - order[slot]) % inner_n).wait_recv()

        def z_start(r, carry, wave=wave):
            z_copy(wave, r).start()
            return carry

        lax.fori_loop(1, outer_n, z_start, 0)
        for slot in range(low, high):
            recv2[o, slot] = recv1[slot - 1, o]
    t_all().wait_recv()
    for slot in turned:
        turn_copy(slot, order[slot]).start()
    def spread(slot):
        place = at_inner(order[slot])
        for source in range(outer_n):
            row = pl.multiple_of((source * inner_n + place) * (2 * per), 2 * per)
            signals[pl.ds(row, 2 * per), :] = recv2[source, slot].astype(F32)

    d_all().wait_recv()
    spread(0)
    for wave, (low, high) in enumerate(waves):
        z_all(wave).wait_recv()
        for slot in range(low, high):
            spread(slot)
    for slot in turned:
        turn_copy(slot, inner_n - order[slot]).wait_recv()
        spread(slot)

    q_start()
    padded = twist_ref.shape[1]
    cos_twist, sin_twist = twist_ref[0], twist_ref[1]
    own_gains = gains[pl.ds(pl.multiple_of(o * per, per), per), :]

    def wide(table, times):
        return jnp.concatenate([table] * times, axis=1)

    def convolve(first):
        both = [
            signals[pl.ds(channel + kind * per, slabs, stride=2 * per), :]
            for channel in (first, first + 1)
            for kind in range(2)
        ]
        x = jnp.concatenate([b.astype(BF16) for b in both], axis=1)
        y = dot(section_ref[...], jnp.concatenate([x, x], axis=0))
        real, imag = y[:padded], y[padded:]
        cos4, sin4 = wide(cos_twist, 4), wide(sin_twist, 4)
        turned_real = real * cos4 + imag * sin4
        turned_imag = imag * cos4 - real * sin4
        stacked = jnp.concatenate(
            [
                jnp.concatenate([t[:, n * tok : (n + 1) * tok] for t in (turned_real, turned_imag)], axis=1)
                for n in range(4)
            ],
            axis=0,
        )
        spec = dot3(stacked, forth_ref)
        prods = []
        for n in range(2):
            a = spec[2 * n * padded : (2 * n + 1) * padded]
            b = spec[(2 * n + 1) * padded : (2 * n + 2) * padded]
            ar, ai, br, bi = a[:, :tok], a[:, tok:], b[:, :tok], b[:, tok:]
            prods.append(jnp.concatenate([ar * br - ai * bi, ar * bi + ai * br], axis=1))
        ret = dot3(jnp.concatenate(prods, axis=0), inverse_ref)
        ups = []
        for n in range(2):
            r = ret[n * padded : (n + 1) * padded]
            rr, ri = r[:, :tok], r[:, tok:]
            ups.append(
                jnp.concatenate([rr * cos_twist - ri * sin_twist, ri * cos_twist + rr * sin_twist], axis=0)
            )
        high, low = halves(jnp.concatenate(ups, axis=1))
        conv = dot(back_ref[0], high) + (dot(back_ref[1], high) + dot(back_ref[0], low))
        mixed = [
            conv[:, n * tok : (n + 1) * tok] + own_gains[first + n : first + n + 1] * both[2 * n] for n in range(2)
        ]
        return jnp.concatenate([m.reshape(outer_n, inner_n, tok) for m in mixed], axis=1).astype(BF16)

    def part_rows(h):
        return pl.ds(h * each * inner_n, each * inner_n)

    def b_copy(h, r):
        return pltpu.make_async_remote_copy(
            src_ref=send2.at[at_outer(r), part_rows(h)], dst_ref=recv3.at[o, part_rows(h)],
            send_sem=b_send.at[h, r], recv_sem=b_recv.at[h, outer_n - r],
            device_id={"outer": at_outer(r)}, device_id_type=MESH,
        )

    def b_arrival(h, r):
        here = recv3.at[at_outer(r), part_rows(h)]
        return pltpu.make_async_remote_copy(
            src_ref=here, dst_ref=here, send_sem=b_send.at[h, r], recv_sem=b_recv.at[h, r],
            device_id={"outer": at_outer(r)}, device_id_type=MESH,
        )

    for h in range(parts):
        for pair in range(h * each // 2, (h + 1) * each // 2):
            send2[:, pl.ds(pair * 2 * inner_n, 2 * inner_n), :] = convolve(2 * pair)

        def b_start(r, carry, h=h):
            b_copy(h, r).start()
            return carry

        lax.fori_loop(1, outer_n, b_start, 0)
    recv3[o] = send2[o]

    for d in range(1, inner_n):
        q_copy(inner_n - d).wait_recv()
    for slab in range(inner_n):
        folded[pl.ds(slab * block, block), :] = q_recv[slab].astype(F32).T
        for cc in range(per):
            gate_q[cc, slab] = folded[pl.ds(slab * block + cc, outer_n, stride=per), :]

    def x_copy(h, d):
        return pltpu.make_async_remote_copy(
            src_ref=gx.at[h, at_chan(d)], dst_ref=gated.at[h, chan_n - d, :, i],
            send_sem=x_send.at[h, d], recv_sem=x_recv.at[h, chan_n - d],
            device_id={"chan": at_chan(d)}, device_id_type=MESH,
        )

    longest = inner_n // 2
    OWN, REST, WHOLE = 0, 1, 2

    def reach(way, h):
        return longest if (h + way) % 2 == 0 else inner_n - 1 - longest

    def g_copy(way, h, r, which, arrival=False):
        step = 1 if way == 0 else inner_n - 1
        source = at_inner((inner_n - step) * (r if arrival else r - 1) % inner_n)
        groups = (pl.ds(0, 1), pl.ds(1, chan_n - 1), pl.ds(0, chan_n))[which]
        held = gated.at[h, groups, :, source]
        place = 0 if which == OWN else r
        return pltpu.make_async_remote_copy(
            src_ref=held, dst_ref=held,
            send_sem=g_send.at[way, h, place], recv_sem=g_recv.at[way, h, place],
            device_id={"inner": at_inner(step)}, device_id_type=MESH,
        )

    for h in range(parts):

        def b_wait(r, carry, h=h):
            b_arrival(h, r).wait_recv()
            return carry

        lax.fori_loop(1, outer_n, b_wait, 0)
        count = each * inner_n
        first = h * outer_n * count
        for source in range(outer_n):
            conv_rows[pl.ds(first + source * count, count), :] = recv3[source, part_rows(h), :].astype(F32)
        for e in range(each):
            cc = h * each + e
            for slab in range(inner_n):
                conv = conv_rows[pl.ds(first + e * inner_n + slab, outer_n, stride=count), :]
                value = (gate_q[cc, slab] * conv).astype(BF16)
                gx[h, slab // near, e, :, pl.ds(slab % near * tok, tok)] = value
        for d in range(1, chan_n):
            x_copy(h, d).start()
        gated[h, 0, :, i] = gx[h, c]
        for way in range(2):
            g_copy(way, h, 1, OWN).start()

    events = []
    for h in range(parts):
        for r in range(1, longest + 2):
            events.append((RING_LAG * h + r, h, r))
    for count, (_, h, r) in enumerate(sorted(events)):
        if count == PASS_AT:
            for d in range(1, chan_n):
                for n in range(spans):
                    w_copy(chan_n - d, n).wait_recv()
                f_copy(d, core).start()
        if r == 1:
            for d in range(1, chan_n):
                x_copy(h, chan_n - d).wait_recv()
        for way in range(2):
            if r == 2:
                g_copy(way, h, 1, OWN, arrival=True).wait_recv()
            if 1 < r <= reach(way, h) + 1:
                g_copy(way, h, r - 1, REST if r == 2 else WHOLE, arrival=True).wait_recv()
            if r <= reach(way, h):
                g_copy(way, h, r, REST if r == 1 else WHOLE).start()
        if r == longest + 1:
            if h == 0:
                for d in range(1, chan_n):
                    f_copy(d, 1 - core).wait_recv()
            part = None
            for group in range(chan_n):
                left, right = weights[group, h], gated[h, group].reshape(each * slabs, near * tok)
                term = dot(left, right)
                part = term if part is None else part + term
            if h < parts - 1:
                total[...] = part if h == 0 else total[...] + part
            else:
                out_ref[...] = (total[...] + part).T.astype(BF16)

    d_all().wait_send()
    t_all().wait_send()
    for slot in turned:
        turn_copy(slot, order[slot]).wait_send()
    for slot in range(1, passed + 1):
        y_copy(slot, order[slot]).wait_send()
    for wave in range(len(waves)):
        z_all(wave).wait_send()
    for d in range(1, inner_n):
        q_copy(d).wait_send()

    def sent(r, carry):
        for h in range(parts):
            b_copy(h, r).wait_send()
        return carry

    lax.fori_loop(1, outer_n, sent, 0)
    for d in range(1, chan_n):
        for n in range(spans):
            w_copy(d, n).wait_send()
        f_copy(d, core).wait_send()
        for h in range(parts):
            x_copy(h, d).wait_send()
    for h in range(parts):
        for way in range(2):
            g_copy(way, h, 1, OWN).wait_send()
            for r in range(1, reach(way, h) + 1):
                g_copy(way, h, r, REST if r == 1 else WHOLE).wait_send()


def local(q_stream, k_stream, v_stream, filter_taps, skip_gain, out_weight):
    tok, chans = k_stream.shape
    outer_n, inner_n, chan_n = (lax.axis_size(a) for a in ("outer", "inner", "chan"))
    slabs = outer_n * inner_n
    per = chans // slabs
    block = outer_n * per
    width = out_weight.shape[1]
    coarse = inner_n * tok
    piece = coarse // chan_n
    held = (*tables(slabs, tok), pick_table(outer_n, per))
    parts = PARTS
    each = per // parts
    lanes = min(width, 128)
    sizes = (outer_n, inner_n, chan_n, tok, per, parts)
    spans = width // lanes
    dma = pltpu.SemaphoreType.DMA
    hbm = pl.BlockSpec(memory_space=pltpu.HBM)
    return pl.pallas_call(
        functools.partial(kernel, sizes),
        out_shape=jax.ShapeDtypeStruct((piece, width), BF16),
        in_specs=[hbm] * 12,
        out_specs=pl.BlockSpec(memory_space=pltpu.VMEM),
        scratch_shapes=[
            pltpu.VMEM((tok, chans), BF16),
            pltpu.VMEM((tok, chans), BF16),
            pltpu.VMEM((tok, chans), BF16),
            pltpu.VMEM((1, chans), F32),
            pltpu.VMEM((chans, width), BF16),
            *(pltpu.VMEM(t.shape, t.dtype) for t in held),
            pltpu.VMEM((inner_n, outer_n, 2 * per, tok), BF16),
            pltpu.VMEM((inner_n - 3, outer_n, 2 * per, tok), BF16),
            pltpu.VMEM((2, outer_n, 2 * per, tok), BF16),
            pltpu.VMEM((outer_n, inner_n, 2 * per, tok), BF16),
            pltpu.VMEM((slabs * 2 * per, tok), F32),
            pltpu.VMEM((outer_n, per * inner_n, tok), BF16),
            pltpu.VMEM((outer_n, per * inner_n, tok), BF16),
            pltpu.VMEM((outer_n * per * inner_n, tok), F32),
            pltpu.VMEM((inner_n, tok, block), BF16),
            pltpu.VMEM((block, tok), F32),
            pltpu.VMEM((inner_n * block, tok), F32),
            pltpu.VMEM((per, inner_n, outer_n, tok), F32),
            pltpu.VMEM((parts, chan_n, each, outer_n, piece), BF16),
            pltpu.VMEM((parts, chan_n, each, inner_n, outer_n, piece), BF16),
            pltpu.VMEM((width // lanes, chans, lanes), F32),
            pltpu.VMEM((chan_n, parts, width, each * slabs), BF16),
            pltpu.VMEM((width, piece), F32),
            dma((12,)),
            dma((inner_n,)),
            dma((inner_n,)),
            dma((inner_n // 2 - 1,)),
            dma((inner_n // 2 - 1,)),
            dma((1,)),
            dma((1,)),
            dma((inner_n,)),
            dma((inner_n,)),
            dma((inner_n,)),
            dma((inner_n,)),
            dma((parts, outer_n)),
            dma((parts, outer_n)),
            dma((parts, chan_n)),
            dma((parts, chan_n)),
            dma((2, parts, inner_n // 2 + 1)),
            dma((2, parts, inner_n // 2 + 1)),
            dma((chan_n, spans)),
            dma((chan_n, spans)),
            dma((chan_n,)),
            dma((chan_n,)),
        ],
        compiler_params=pltpu.CompilerParams(
            collective_id=0, has_side_effects=True, vmem_limit_bytes=60 * 1024 * 1024
        ),
    )(q_stream, k_stream, v_stream, filter_taps, skip_gain[None, :], out_weight, *(jnp.asarray(t) for t in held))


def solution(mesh):
    return jax.shard_map(
        local,
        mesh=mesh,
        in_specs=(
            P(("outer", "inner"), "chan"),
            P(("outer", "inner"), "chan"),
            P(("outer", "inner"), "chan"),
            P(("outer", "inner"), "chan"),
            P("chan"),
            P("chan", "inner"),
        ),
        out_specs=P(("outer", "chan"), "inner"),
        check_vma=False,
    )
```

```python
import functools

import jax
import jax.numpy as jnp
import numpy as np
from jax import lax
from jax.experimental import pallas as pl
from jax.experimental.pallas import tpu as pltpu
from jax.sharding import PartitionSpec as P

MESH = pl.DeviceIdType.MESH
F32 = jnp.float32
BF16 = jnp.bfloat16
PARTS = 4
RING_LAG = 0.3
PASS_AT = 3


def split_table(values):
    high = values.astype(np.float32).astype(jnp.bfloat16)
    low = (values - high.astype(np.float64)).astype(np.float32).astype(jnp.bfloat16)
    return high, low


@functools.lru_cache(maxsize=None)
def tables(slabs, tok):
    coarse = 2 * slabs
    total = coarse * tok
    rows = slabs + 1
    padded = -(-rows // 16) * 16
    k = np.arange(padded)
    live = (k < rows).astype(np.float64)
    angle = 2 * np.pi * ((k[:, None] * np.arange(slabs)[None, :]) % coarse) / coarse
    cos, sin = np.cos(angle) * live[:, None], np.sin(angle) * live[:, None]
    section = np.concatenate(split_table(np.concatenate([cos, -sin], axis=0)), axis=1)
    weight = np.where((k == 0) | (k == slabs), 1.0, 2.0) / total
    back = np.concatenate([(cos * weight[:, None]).T, (-sin * weight[:, None]).T], axis=1)
    back = np.stack(split_table(back))
    turn = 2 * np.pi * ((k[:, None] * np.arange(tok)[None, :]) % total) / total
    twist = np.stack([np.cos(turn), np.sin(turn)]).astype(np.float32)
    m = np.arange(tok)
    fine = 2 * np.pi * ((m[:, None] * m[None, :]) % tok) / tok
    c, s = np.cos(fine), np.sin(fine)
    forth = np.stack(split_table(np.block([[c, -s], [s, c]])))
    inverse = np.stack(split_table(np.block([[c, s], [-s, c]])))
    return section, twist, forth, inverse, back


def pick_table(outer_n, per):
    block = outer_n * per
    device, signal, channel = np.meshgrid(np.arange(outer_n), np.arange(2), np.arange(per), indexing="ij")
    column = (signal * block + device * per + channel).reshape(-1)
    return (column[:, None] == np.arange(2 * block)[None, :]).astype(np.float32).astype(jnp.bfloat16)


def dot(a, b):
    return jnp.dot(a, b, preferred_element_type=F32)


def halves(x):
    high = x.astype(BF16)
    return high, (x - high.astype(F32)).astype(BF16)


def dot3(x, table):
    high, low = halves(x)
    return dot(high, table[0]) + (dot(high, table[1]) + dot(low, table[0]))


def path_order(n):
    order = [0]
    for d in range(1, n // 2 - 1):
        order += [d, n - d]
    return order + [n // 2, n // 2 - 1, n // 2 + 1]


def kernel(
    sizes,
    q_hbm, k_hbm, v_hbm, taps_hbm, skip_hbm, w_hbm,
    section_hbm, twist_hbm, forth_hbm, inverse_hbm, back_hbm, pick_hbm,
    out_hbm,
    k_buf, v_buf, taps_buf, skip_ref, w_buf, section_ref, twist_ref, forth_ref, inverse_ref, back_ref, pick_ref,
    send1, recv1, middle, recv2, signals, send2, recv3, conv_rows, q_recv, gains, folded, gate_q,
    gx, gated, w_rows, weights, total, out_buf,
    load_sem, out_sem, y_send, y_recv, z_send, z_recv, t_send, t_recv, d_send, d_recv, q_send, q_recv_sem, b_send, b_recv, x_send, x_recv,
    g_send, g_recv, w_send, w_recv, f_send, f_recv,
):
    outer_n, inner_n, chan_n, tok, per, parts = sizes
    slabs = outer_n * inner_n
    block = outer_n * per
    each = per // parts
    o, i, c = lax.axis_index("outer"), lax.axis_index("inner"), lax.axis_index("chan")
    order = path_order(inner_n)
    near = inner_n // chan_n
    passed = inner_n - 3
    waves = [(low, min(low + 2, passed + 1)) for low in range(1, passed + 1, 2)]
    turned = (passed + 1, passed + 2)
    core = lax.rem(o, 2)
    sibling = o + 1 - 2 * core

    def at_inner(d):
        return lax.rem(i + d, inner_n)

    def at_outer(r):
        return lax.rem(o + r, outer_n)

    def at_chan(d):
        return lax.rem(c + d, chan_n)

    def cols(index):
        return pl.ds(pl.multiple_of(index * block, block), block)

    barrier = pltpu.get_barrier_semaphore()
    for d in range(1, inner_n):
        pl.semaphore_signal(barrier, inc=1, device_id={"inner": at_inner(d)}, device_id_type=MESH)
    for r in range(1, outer_n):
        pl.semaphore_signal(barrier, inc=1, device_id={"outer": at_outer(r)}, device_id_type=MESH)
    for d in range(1, chan_n):
        pl.semaphore_signal(barrier, inc=1, device_id={"chan": at_chan(d)}, device_id_type=MESH)

    loads = [
        pltpu.make_async_copy(k_hbm, k_buf, load_sem.at[0]),
        pltpu.make_async_copy(v_hbm, v_buf, load_sem.at[1]),
        pltpu.make_async_copy(taps_hbm, taps_buf, load_sem.at[2]),
        pltpu.make_async_copy(pick_hbm, pick_ref, load_sem.at[11]),
        pltpu.make_async_copy(q_hbm.at[:, cols(i)], q_recv.at[i], load_sem.at[3]),
        pltpu.make_async_copy(skip_hbm, skip_ref, load_sem.at[4]),
        pltpu.make_async_copy(section_hbm, section_ref, load_sem.at[5]),
        pltpu.make_async_copy(twist_hbm, twist_ref, load_sem.at[6]),
        pltpu.make_async_copy(forth_hbm, forth_ref, load_sem.at[7]),
        pltpu.make_async_copy(inverse_hbm, inverse_ref, load_sem.at[8]),
        pltpu.make_async_copy(back_hbm, back_ref, load_sem.at[9]),
        pltpu.make_async_copy(w_hbm, w_buf, load_sem.at[10]),
    ]
    for load in loads:
        load.start()
    pl.semaphore_wait(barrier, inner_n + outer_n + chan_n - 3)
    for load in loads[:4]:
        load.wait()

    def pack(index):
        span = cols(index)
        product = (k_buf[:, span].astype(F32) * v_buf[:, span].astype(F32)).astype(BF16)
        both = jnp.concatenate([product, taps_buf[:, span]], axis=1)
        rows = lax.dot_general(pick_ref[...], both, (((1,), (1,)), ((), ())), preferred_element_type=F32)
        return rows.reshape(outer_n, 2 * per, tok).astype(BF16)

    def d_copy(r):
        return pltpu.make_async_remote_copy(
            src_ref=send1.at[0, at_outer(r)], dst_ref=recv2.at[o, 0], send_sem=d_send.at[0], recv_sem=d_recv.at[0],
            device_id={"outer": at_outer(r)}, device_id_type=MESH,
        )

    def d_all():
        held = recv2.at[pl.ds(0, outer_n - 1), 0]
        return pltpu.make_async_remote_copy(
            src_ref=held, dst_ref=held, send_sem=d_send.at[0], recv_sem=d_recv.at[0],
            device_id={"outer": sibling}, device_id_type=MESH,
        )

    def t_copy(r):
        return pltpu.make_async_remote_copy(
            src_ref=send1.at[pl.ds(turned[0], 2), at_outer(r)], dst_ref=middle.at[:, o],
            send_sem=t_send.at[0], recv_sem=t_recv.at[0],
            device_id={"outer": at_outer(r)}, device_id_type=MESH,
        )

    def t_all():
        held = middle.at[:, pl.ds(0, outer_n - 1)]
        return pltpu.make_async_remote_copy(
            src_ref=held, dst_ref=held, send_sem=t_send.at[0], recv_sem=t_recv.at[0],
            device_id={"outer": sibling}, device_id_type=MESH,
        )

    def turn_copy(slot, d):
        there = order.index((inner_n - d) % inner_n)
        return pltpu.make_async_remote_copy(
            src_ref=middle.at[slot - turned[0]], dst_ref=recv2.at[:, there],
            send_sem=d_send.at[slot], recv_sem=d_recv.at[there],
            device_id={"inner": at_inner(d)}, device_id_type=MESH,
        )

    def y_copy(slot, d):
        there = order.index((inner_n - d) % inner_n)
        return pltpu.make_async_remote_copy(
            src_ref=send1.at[slot], dst_ref=recv1.at[there - 1], send_sem=y_send.at[slot], recv_sem=y_recv.at[there],
            device_id={"inner": at_inner(d)}, device_id_type=MESH,
        )

    def z_copy(wave, r):
        low, high = waves[wave]
        return pltpu.make_async_remote_copy(
            src_ref=recv1.at[pl.ds(low - 1, high - low), at_outer(r)],
            dst_ref=recv2.at[o, pl.ds(low, high - low)],
            send_sem=z_send.at[wave], recv_sem=z_recv.at[wave],
            device_id={"outer": at_outer(r)}, device_id_type=MESH,
        )

    def z_all(wave):
        low, high = waves[wave]
        held = recv2.at[pl.ds(0, outer_n - 1), pl.ds(low, high - low)]
        return pltpu.make_async_remote_copy(
            src_ref=held, dst_ref=held, send_sem=z_send.at[wave], recv_sem=z_recv.at[wave],
            device_id={"outer": sibling}, device_id_type=MESH,
        )

    def q_copy(d):
        return pltpu.make_async_remote_copy(
            src_ref=q_hbm.at[:, cols(at_inner(d))], dst_ref=q_recv.at[i],
            send_sem=q_send.at[d], recv_sem=q_recv_sem.at[inner_n - d],
            device_id={"inner": at_inner(d)}, device_id_type=MESH,
        )

    def q_start():
        for d in order[1:]:
            q_copy(d).start()

    def y_go(slot):
        send1[slot] = pack(at_inner(order[slot]))
        y_copy(slot, order[slot]).start()

    for slot in range(1, passed):
        y_go(slot)
    for slot in turned:
        send1[slot] = pack(at_inner(order[slot]))

    def t_start(r, carry):
        t_copy(r).start()
        return carry

    def d_start(r, carry):
        d_copy(r).start()
        return carry

    lax.fori_loop(1, outer_n, t_start, 0)
    middle[:, o] = send1[turned[0] : turned[1] + 1, o]
    send1[0] = pack(i)
    lax.fori_loop(1, outer_n, d_start, 0)
    recv2[o, 0] = send1[0, o]
    y_go(passed)

    for load in loads[4:]:
        load.wait()
    mine = pl.ds(core * (parts // 2), parts // 2)
    spans = w_rows.shape[0]

    def span_of(n):
        return pl.ds(n * w_rows.shape[2], w_rows.shape[2])

    def w_copy(d, n):
        return pltpu.make_async_remote_copy(
            src_ref=weights.at[0, mine, span_of(n)], dst_ref=weights.at[chan_n - d, mine, span_of(n)],
            send_sem=w_send.at[d, n], recv_sem=w_recv.at[chan_n - d, n],
            device_id={"chan": at_chan(d)}, device_id_type=MESH,
        )

    def f_copy(d, half):
        held = weights.at[d, pl.ds(half * (parts // 2), parts // 2)]
        return pltpu.make_async_remote_copy(
            src_ref=held, dst_ref=held, send_sem=f_send.at[d], recv_sem=f_recv.at[d],
            device_id={"outer": sibling}, device_id_type=MESH,
        )

    def w_part(n):
        w_rows[n] = w_buf[:, span_of(n)].astype(F32)
        for cc in range(per):
            rows = w_rows[n, pl.ds(cc, slabs, stride=per), :]
            weights[0, cc // each, span_of(n), pl.ds(cc % each * slabs, slabs)] = rows.T.astype(BF16)
        for d in range(1, chan_n):
            w_copy(d, n).start()

    for n in range(spans):
        w_part(n)
    gains[...] = jnp.broadcast_to(skip_ref[:, cols(i)], (tok, block)).T

    for wave, (low, high) in enumerate(waves):
        for slot in range(low, high):
            y_copy(slot, (inner_n - order[slot]) % inner_n).wait_recv()

        def z_start(r, carry, wave=wave):
            z_copy(wave, r).start()
            return carry

        lax.fori_loop(1, outer_n, z_start, 0)
        for slot in range(low, high):
            recv2[o, slot] = recv1[slot - 1, o]
    t_all().wait_recv()
    for slot in turned:
        turn_copy(slot, order[slot]).start()
    def spread(slot):
        place = at_inner(order[slot])
        for source in range(outer_n):
            row = pl.multiple_of((source * inner_n + place) * (2 * per), 2 * per)
            signals[pl.ds(row, 2 * per), :] = recv2[source, slot].astype(F32)

    d_all().wait_recv()
    spread(0)
    for wave, (low, high) in enumerate(waves):
        z_all(wave).wait_recv()
        for slot in range(low, high):
            spread(slot)
    for slot in turned:
        turn_copy(slot, inner_n - order[slot]).wait_recv()
        spread(slot)

    q_start()
    padded = twist_ref.shape[1]
    cos_twist, sin_twist = twist_ref[0], twist_ref[1]
    own_gains = gains[pl.ds(pl.multiple_of(o * per, per), per), :]

    def wide(table, times):
        return jnp.concatenate([table] * times, axis=1)

    def convolve(first):
        both = [
            signals[pl.ds(channel + kind * per, slabs, stride=2 * per), :]
            for channel in (first, first + 1)
            for kind in range(2)
        ]
        x = jnp.concatenate([b.astype(BF16) for b in both], axis=1)
        y = dot(section_ref[...], jnp.concatenate([x, x], axis=0))
        real, imag = y[:padded], y[padded:]
        cos4, sin4 = wide(cos_twist, 4), wide(sin_twist, 4)
        turned_real = real * cos4 + imag * sin4
        turned_imag = imag * cos4 - real * sin4
        stacked = jnp.concatenate(
            [
                jnp.concatenate([t[:, n * tok : (n + 1) * tok] for t in (turned_real, turned_imag)], axis=1)
                for n in range(4)
            ],
            axis=0,
        )
        spec = dot3(stacked, forth_ref)
        prods = []
        for n in range(2):
            a = spec[2 * n * padded : (2 * n + 1) * padded]
            b = spec[(2 * n + 1) * padded : (2 * n + 2) * padded]
            ar, ai, br, bi = a[:, :tok], a[:, tok:], b[:, :tok], b[:, tok:]
            prods.append(jnp.concatenate([ar * br - ai * bi, ar * bi + ai * br], axis=1))
        ret = dot3(jnp.concatenate(prods, axis=0), inverse_ref)
        ups = []
        for n in range(2):
            r = ret[n * padded : (n + 1) * padded]
            rr, ri = r[:, :tok], r[:, tok:]
            ups.append(
                jnp.concatenate([rr * cos_twist - ri * sin_twist, ri * cos_twist + rr * sin_twist], axis=0)
            )
        high, low = halves(jnp.concatenate(ups, axis=1))
        conv = dot(back_ref[0], high) + (dot(back_ref[1], high) + dot(back_ref[0], low))
        mixed = [
            conv[:, n * tok : (n + 1) * tok] + own_gains[first + n : first + n + 1] * both[2 * n] for n in range(2)
        ]
        return jnp.concatenate([m.reshape(outer_n, inner_n, tok) for m in mixed], axis=1).astype(BF16)

    def part_rows(h):
        return pl.ds(h * each * inner_n, each * inner_n)

    def b_copy(h, r):
        return pltpu.make_async_remote_copy(
            src_ref=send2.at[at_outer(r), part_rows(h)], dst_ref=recv3.at[o, part_rows(h)],
            send_sem=b_send.at[h, r], recv_sem=b_recv.at[h, outer_n - r],
            device_id={"outer": at_outer(r)}, device_id_type=MESH,
        )

    def b_arrival(h, r):
        here = recv3.at[at_outer(r), part_rows(h)]
        return pltpu.make_async_remote_copy(
            src_ref=here, dst_ref=here, send_sem=b_send.at[h, r], recv_sem=b_recv.at[h, r],
            device_id={"outer": at_outer(r)}, device_id_type=MESH,
        )

    for h in range(parts):
        for pair in range(h * each // 2, (h + 1) * each // 2):
            send2[:, pl.ds(pair * 2 * inner_n, 2 * inner_n), :] = convolve(2 * pair)

        def b_start(r, carry, h=h):
            b_copy(h, r).start()
            return carry

        lax.fori_loop(1, outer_n, b_start, 0)
    recv3[o] = send2[o]

    for d in range(1, inner_n):
        q_copy(inner_n - d).wait_recv()
    for slab in range(inner_n):
        folded[pl.ds(slab * block, block), :] = q_recv[slab].astype(F32).T
        for cc in range(per):
            gate_q[cc, slab] = folded[pl.ds(slab * block + cc, outer_n, stride=per), :]

    def x_copy(h, d):
        return pltpu.make_async_remote_copy(
            src_ref=gx.at[h, at_chan(d)], dst_ref=gated.at[h, chan_n - d, :, i],
            send_sem=x_send.at[h, d], recv_sem=x_recv.at[h, chan_n - d],
            device_id={"chan": at_chan(d)}, device_id_type=MESH,
        )

    longest = inner_n // 2
    OWN, REST, WHOLE = 0, 1, 2

    def reach(way, h):
        return longest if (h + way) % 2 == 0 else inner_n - 1 - longest

    def g_copy(way, h, r, which, arrival=False):
        step = 1 if way == 0 else inner_n - 1
        source = at_inner((inner_n - step) * (r if arrival else r - 1) % inner_n)
        groups = (pl.ds(0, 1), pl.ds(1, chan_n - 1), pl.ds(0, chan_n))[which]
        held = gated.at[h, groups, :, source]
        place = 0 if which == OWN else r
        return pltpu.make_async_remote_copy(
            src_ref=held, dst_ref=held,
            send_sem=g_send.at[way, h, place], recv_sem=g_recv.at[way, h, place],
            device_id={"inner": at_inner(step)}, device_id_type=MESH,
        )

    for h in range(parts):

        def b_wait(r, carry, h=h):
            b_arrival(h, r).wait_recv()
            return carry

        lax.fori_loop(1, outer_n, b_wait, 0)
        count = each * inner_n
        first = h * outer_n * count
        for source in range(outer_n):
            conv_rows[pl.ds(first + source * count, count), :] = recv3[source, part_rows(h), :].astype(F32)
        for e in range(each):
            cc = h * each + e
            for slab in range(inner_n):
                conv = conv_rows[pl.ds(first + e * inner_n + slab, outer_n, stride=count), :]
                value = (gate_q[cc, slab] * conv).astype(BF16)
                gx[h, slab // near, e, :, pl.ds(slab % near * tok, tok)] = value
        for d in range(1, chan_n):
            x_copy(h, d).start()
        gated[h, 0, :, i] = gx[h, c]
        for way in range(2):
            g_copy(way, h, 1, OWN).start()

    def out_copy(low, step):
        span = pl.ds(low, step)
        return pltpu.make_async_copy(out_buf.at[:, span], out_hbm.at[:, span], out_sem.at[low // step])

    events = []
    for h in range(parts):
        for r in range(1, longest + 2):
            events.append((RING_LAG * h + r, h, r))
    for count, (_, h, r) in enumerate(sorted(events)):
        if count == PASS_AT:
            for d in range(1, chan_n):
                for n in range(spans):
                    w_copy(chan_n - d, n).wait_recv()
                f_copy(d, core).start()
        if r == 1:
            for d in range(1, chan_n):
                x_copy(h, chan_n - d).wait_recv()
        for way in range(2):
            if r == 2:
                g_copy(way, h, 1, OWN, arrival=True).wait_recv()
            if 1 < r <= reach(way, h) + 1:
                g_copy(way, h, r - 1, REST if r == 2 else WHOLE, arrival=True).wait_recv()
            if r <= reach(way, h):
                g_copy(way, h, r, REST if r == 1 else WHOLE).start()
        if r == longest + 1:
            if h == 0:
                for d in range(1, chan_n):
                    f_copy(d, 1 - core).wait_recv()
            width = total.shape[0]
            step = width if h < parts - 1 else width // 2
            for low in range(0, width, step):
                span = pl.ds(low, step)
                part = None
                for group in range(chan_n):
                    left, right = weights[group, h, span], gated[h, group].reshape(each * slabs, near * tok)
                    term = dot(left, right)
                    part = term if part is None else part + term
                if h < parts - 1:
                    total[...] = part if h == 0 else total[...] + part
                else:
                    out_buf[:, span] = (total[span, :] + part).T.astype(BF16)
                    out_copy(low, step).start()

    d_all().wait_send()
    t_all().wait_send()
    for slot in turned:
        turn_copy(slot, order[slot]).wait_send()
    for slot in range(1, passed + 1):
        y_copy(slot, order[slot]).wait_send()
    for wave in range(len(waves)):
        z_all(wave).wait_send()
    for d in range(1, inner_n):
        q_copy(d).wait_send()

    def sent(r, carry):
        for h in range(parts):
            b_copy(h, r).wait_send()
        return carry

    lax.fori_loop(1, outer_n, sent, 0)
    for d in range(1, chan_n):
        for n in range(spans):
            w_copy(d, n).wait_send()
        f_copy(d, core).wait_send()
        for h in range(parts):
            x_copy(h, d).wait_send()
    for h in range(parts):
        for way in range(2):
            g_copy(way, h, 1, OWN).wait_send()
            for r in range(1, reach(way, h) + 1):
                g_copy(way, h, r, REST if r == 1 else WHOLE).wait_send()
    for half in range(2):
        out_copy(half * (total.shape[0] // 2), total.shape[0] // 2).wait()


def local(q_stream, k_stream, v_stream, filter_taps, skip_gain, out_weight):
    tok, chans = k_stream.shape
    outer_n, inner_n, chan_n = (lax.axis_size(a) for a in ("outer", "inner", "chan"))
    slabs = outer_n * inner_n
    per = chans // slabs
    block = outer_n * per
    width = out_weight.shape[1]
    coarse = inner_n * tok
    piece = coarse // chan_n
    held = (*tables(slabs, tok), pick_table(outer_n, per))
    parts = PARTS
    each = per // parts
    lanes = min(width, 128)
    sizes = (outer_n, inner_n, chan_n, tok, per, parts)
    spans = width // lanes
    dma = pltpu.SemaphoreType.DMA
    hbm = pl.BlockSpec(memory_space=pltpu.HBM)
    return pl.pallas_call(
        functools.partial(kernel, sizes),
        out_shape=jax.ShapeDtypeStruct((piece, width), BF16),
        in_specs=[hbm] * 12,
        out_specs=hbm,
        scratch_shapes=[
            pltpu.VMEM((tok, chans), BF16),
            pltpu.VMEM((tok, chans), BF16),
            pltpu.VMEM((tok, chans), BF16),
            pltpu.VMEM((1, chans), F32),
            pltpu.VMEM((chans, width), BF16),
            *(pltpu.VMEM(t.shape, t.dtype) for t in held),
            pltpu.VMEM((inner_n, outer_n, 2 * per, tok), BF16),
            pltpu.VMEM((inner_n - 3, outer_n, 2 * per, tok), BF16),
            pltpu.VMEM((2, outer_n, 2 * per, tok), BF16),
            pltpu.VMEM((outer_n, inner_n, 2 * per, tok), BF16),
            pltpu.VMEM((slabs * 2 * per, tok), F32),
            pltpu.VMEM((outer_n, per * inner_n, tok), BF16),
            pltpu.VMEM((outer_n, per * inner_n, tok), BF16),
            pltpu.VMEM((outer_n * per * inner_n, tok), F32),
            pltpu.VMEM((inner_n, tok, block), BF16),
            pltpu.VMEM((block, tok), F32),
            pltpu.VMEM((inner_n * block, tok), F32),
            pltpu.VMEM((per, inner_n, outer_n, tok), F32),
            pltpu.VMEM((parts, chan_n, each, outer_n, piece), BF16),
            pltpu.VMEM((parts, chan_n, each, inner_n, outer_n, piece), BF16),
            pltpu.VMEM((width // lanes, chans, lanes), F32),
            pltpu.VMEM((chan_n, parts, width, each * slabs), BF16),
            pltpu.VMEM((width, piece), F32),
            pltpu.VMEM((piece, width), BF16),
            dma((12,)),
            dma((2,)),
            dma((inner_n,)),
            dma((inner_n,)),
            dma((inner_n // 2 - 1,)),
            dma((inner_n // 2 - 1,)),
            dma((1,)),
            dma((1,)),
            dma((inner_n,)),
            dma((inner_n,)),
            dma((inner_n,)),
            dma((inner_n,)),
            dma((parts, outer_n)),
            dma((parts, outer_n)),
            dma((parts, chan_n)),
            dma((parts, chan_n)),
            dma((2, parts, inner_n // 2 + 1)),
            dma((2, parts, inner_n // 2 + 1)),
            dma((chan_n, spans)),
            dma((chan_n, spans)),
            dma((chan_n,)),
            dma((chan_n,)),
        ],
        compiler_params=pltpu.CompilerParams(
            collective_id=0, has_side_effects=True, vmem_limit_bytes=60 * 1024 * 1024
        ),
    )(q_stream, k_stream, v_stream, filter_taps, skip_gain[None, :], out_weight, *(jnp.asarray(t) for t in held))


def solution(mesh):
    return jax.shard_map(
        local,
        mesh=mesh,
        in_specs=(
            P(("outer", "inner"), "chan"),
            P(("outer", "inner"), "chan"),
            P(("outer", "inner"), "chan"),
            P(("outer", "inner"), "chan"),
            P("chan"),
            P("chan", "inner"),
        ),
        out_specs=P(("outer", "chan"), "inner"),
        check_vma=False,
    )
```
